32 devices in a mesh: rep: 4 (over y, x), shard: 8 (over z, core).
Axes of the slice: x: 2, y: 2, z: 4, core: 2. Of those that a mesh axis runs over, the one named last changes fastest.
Arguments:
- tokens_in: bfloat16 [8, 2048, 1536], P('shard', 'rep'), may hold values from -6 to 6
- lengths: int32 [8], P('shard'), may hold values from 512 to 2048, as said below
- cotangent: bfloat16 [8, 2048, 1536], P('shard', 'rep'), may hold values from -6 to 6
- attn_norm: bfloat16 [1536], P('shard'), may hold values from 0.5 to 1.5
- query_proj: bfloat16 [1536, 1536], P('shard'), may hold values from -0.15625 to 0.15625
- key_proj: bfloat16 [1536, 128], P('shard'), may hold values from -0.15625 to 0.15625
- value_proj: bfloat16 [1536, 128], P('shard'), may hold values from -0.15625 to 0.15625
- attn_out: bfloat16 [1536, 1536], P('shard'), may hold values from -2.5 to 2.5
- first_norm: bfloat16 [1536], P('shard'), may hold values from 0.5 to 1.5
- first_gate: bfloat16 [1536, 4608], P('shard'), may hold values from -0.15625 to 0.15625
- first_up: bfloat16 [1536, 4608], P('shard'), may hold values from -0.15625 to 0.15625
- first_down: bfloat16 [4608, 1536], P('shard'), may hold values from -0.09375 to 0.09375
- mixer_norm: bfloat16 [1536], P('shard'), may hold values from 0.5 to 1.5
- branch_proj: bfloat16 [1536, 2048], P('shard'), may hold values from -0.15625 to 0.15625
- gated_proj: bfloat16 [1536, 2048], P('shard'), may hold values from -0.15625 to 0.15625
- conv_taps: bfloat16 [2048, 4], P('shard'), may hold values from -3 to 3
- rate_gate: bfloat16 [2048, 128], P('shard'), may hold values from -0.5 to 0.5
- input_gate: bfloat16 [2048, 128], P('shard'), may hold values from -0.5 to 0.5
- decay_rate: bfloat16 [2048], P('shard'), may hold values from 9.727478e-05 to 0.019897461
- mixer_out: bfloat16 [2048, 1536], P('shard'), may hold values from -0.25 to 0.25
- second_norm: bfloat16 [1536], P('shard'), may hold values from 0.5 to 1.5
- second_gate: bfloat16 [1536, 4608], P('shard'), may hold values from -0.15625 to 0.15625
- second_up: bfloat16 [1536, 4608], P('shard'), may hold values from -0.15625 to 0.15625
- second_down: bfloat16 [4608, 1536], P('shard'), may hold values from -0.09375 to 0.09375
Outputs:
- out: bfloat16 [8, 2048, 1536], P('shard', 'rep')
- input_grad: bfloat16 [8, 2048, 1536], P('shard', 'rep')
- grad_attn_norm: float32 [1536], P('shard')
- grad_query_proj: float32 [1536, 1536], P('shard')
- grad_key_proj: float32 [1536, 128], P('shard')
- grad_value_proj: float32 [1536, 128], P('shard')
- grad_attn_out: float32 [1536, 1536], P('shard')
- grad_first_norm: float32 [1536], P('shard')
- grad_first_gate: float32 [1536, 4608], P('shard')
- grad_first_up: float32 [1536, 4608], P('shard')
- grad_first_down: float32 [4608, 1536], P('shard')
- grad_mixer_norm: float32 [1536], P('shard')
- grad_branch_proj: float32 [1536, 2048], P('shard')
- grad_gated_proj: float32 [1536, 2048], P('shard')
- grad_conv_taps: float32 [2048, 4], P('shard')
- grad_rate_gate: float32 [2048, 128], P('shard')
- grad_input_gate: float32 [2048, 128], P('shard')
- grad_decay_rate: float32 [2048], P('shard')
- grad_mixer_out: float32 [2048, 1536], P('shard')
- grad_second_norm: float32 [1536], P('shard')
- grad_second_gate: float32 [1536, 4608], P('shard')
- grad_second_up: float32 [1536, 4608], P('shard')
- grad_second_down: float32 [4608, 1536], P('shard')
The draws below stay inside these ranges and needn't reach their ends.
Inputs may be any that keep to these rules, and one draw needn't show every extreme that they name: `lengths`: valid slots of each sequence; the slots from this length on are padding. One sequence, drawn from the seed, fills all 2048 slots.
All inputs are finite; a program needn't handle non-finite values.
Results may differ from the reference program's by a relative error of at most 0.02.
Values may be sent and summed in bfloat16 or wider, within the bound.
A program may use at most 512 MiB of HBM per device.

```python
import math
import jax
import jax.numpy as jnp
from jax import lax

D = 1536
HEADS = 12
HEAD = 128
WINDOW = 1024
FF = 4608
RNN = 2048
CONV = 4
BLOCKS = 16
SEQ = 2048
SEQS = 8


def draw_lengths(key, part):
    key = jax.random.fold_in(key, 11)
    first_key, second_key = jax.random.split(key)
    drawn = jax.random.randint(first_key, (SEQS,), SEQ // 4, SEQ + 1, dtype=jnp.int32)
    chosen = jax.random.randint(second_key, (), 0, SEQS, dtype=jnp.int32)
    filled = jnp.full((SEQS,), SEQ, dtype=jnp.int32)
    return jnp.where(jnp.arange(SEQS, dtype=jnp.int32) == chosen, filled, drawn).astype(jnp.int32)


def shard_levels(key, extent, cuts, smallest, high):
    loudness, own = 1.0, jax.random.fold_in(key, 6)
    for dim, parts in cuts:
        draws = jnp.exp(jax.random.uniform(jax.random.fold_in(own, dim), (parts,), jnp.float32, smallest / len(cuts), high / len(cuts)))
        loudness = loudness * jnp.repeat(draws, extent[dim] // parts).reshape([-1 if axis == dim else 1 for axis in range(len(extent))])
    return loudness


def bell_draw(own_key, shape, width, bound, pieces=(), kind=jnp.bfloat16):
    values = width * jax.random.normal(own_key, shape, jnp.float32)
    if pieces:
        values = values * shard_levels(own_key, shape, pieces, -0.22, 0.18)
    return jnp.clip(values, -bound, bound).astype(kind)


def setup_inputs(seed: int = 0) -> dict:
    streams_of = jax.random.split(jax.random.key(seed), 25)
    return {
        "tokens_in": bell_draw(streams_of[0], (SEQS, SEQ, D), 1.0, 6.0, ((0, 8), (1, 4))),
        "lengths": draw_lengths(jax.random.fold_in(streams_of[24], 71), 0),
        "cotangent": bell_draw(streams_of[2], (SEQS, SEQ, D), 1.0, 6.0, ((0, 8), (1, 4))),
        "attn_norm": jnp.clip(1.0 + 0.1 * jax.random.normal(streams_of[3], (D,), jnp.float32), 0.5, 1.5).astype(jnp.bfloat16),
        "query_proj": bell_draw(streams_of[4], (D, HEADS * HEAD), D ** -0.5, 0.15625, ((0, 8),)),
        "key_proj": bell_draw(streams_of[5], (D, HEAD), D ** -0.5, 0.15625, ((0, 8),)),
        "value_proj": bell_draw(streams_of[6], (D, HEAD), D ** -0.5, 0.15625, ((0, 8),)),
        "attn_out": bell_draw(streams_of[7], (HEADS * HEAD, D), (HEADS * HEAD * 4 // WINDOW) ** -0.5, 2.5, ((0, 8),)),
        "first_norm": jnp.clip(1.0 + 0.1 * jax.random.normal(streams_of[8], (D,), jnp.float32), 0.5, 1.5).astype(jnp.bfloat16),
        "first_gate": bell_draw(streams_of[9], (D, FF), D ** -0.5, 0.15625, ((0, 8),)),
        "first_up": bell_draw(streams_of[10], (D, FF), D ** -0.5, 0.15625, ((0, 8),)),
        "first_down": bell_draw(streams_of[11], (FF, D), FF ** -0.5, 0.09375, ((0, 8),)),
        "mixer_norm": jnp.clip(1.0 + 0.1 * jax.random.normal(streams_of[12], (D,), jnp.float32), 0.5, 1.5).astype(jnp.bfloat16),
        "branch_proj": bell_draw(streams_of[13], (D, RNN), D ** -0.5, 0.15625, ((0, 8),)),
        "gated_proj": bell_draw(streams_of[14], (D, RNN), D ** -0.5, 0.15625, ((0, 8),)),
        "conv_taps": bell_draw(streams_of[15], (RNN, CONV), CONV ** -0.5, 3.0, ((0, 8),)),
        "rate_gate": bell_draw(streams_of[16], (RNN, RNN // BLOCKS), (RNN // BLOCKS) ** -0.5, 0.5, ((0, 8),)),
        "input_gate": bell_draw(streams_of[17], (RNN, RNN // BLOCKS), (RNN // BLOCKS) ** -0.5, 0.5, ((0, 8),)),
        "decay_rate": jnp.clip(jnp.exp(math.log(0.019897461) - 5.32080765 * jax.random.uniform(streams_of[18], (RNN,), jnp.float32) ** shard_levels(streams_of[18], (RNN,), ((0, 8),), -0.2, 0.2)), 9.72747802734375e-05, 0.019897461).astype(jnp.bfloat16),
        "mixer_out": bell_draw(streams_of[19], (RNN, D), (RNN // 4) ** -0.5, 0.25, ((0, 8),)),
        "second_norm": jnp.clip(1.0 + 0.1 * jax.random.normal(streams_of[20], (D,), jnp.float32), 0.5, 1.5).astype(jnp.bfloat16),
        "second_gate": bell_draw(streams_of[21], (D, FF), D ** -0.5, 0.15625, ((0, 8),)),
        "second_up": bell_draw(streams_of[22], (D, FF), D ** -0.5, 0.15625, ((0, 8),)),
        "second_down": bell_draw(streams_of[23], (FF, D), FF ** -0.5, 0.09375, ((0, 8),)),
    }


EPSILON = 1e-06
HIGHEST = lax.Precision.HIGHEST

@jax.custom_vjp
def low(v):
    return lax.optimization_barrier(v.astype(jnp.bfloat16)).astype(jnp.float32)

@jax.custom_vjp
def low_back(v):
    return v

def low_keep(v):
    return (low(v), None)

def low_pass(kept, grad):
    return (grad,)

def back_keep(v):
    return (v, None)

def back_low(kept, grad):
    return (low(grad),)
low.defvjp(low_keep, low_pass)
low_back.defvjp(back_keep, back_low)

def product(first_op, second_op):
    return jnp.dot(first_op, second_op, precision=HIGHEST)

def rms_norm(values, norm_gain):
    return values * lax.rsqrt(lax.optimization_barrier(jnp.mean(values * values, axis=-1, keepdims=True)) + EPSILON) * norm_gain

def gelu_tanh(values):
    return jax.nn.gelu(values, approximate=True)

def lru_gates(rate_pre, input_pre, decay_w, conv_out):
    log_coef = -8.0 * jax.nn.sigmoid(rate_pre) * decay_w
    lru_coef = jnp.exp(log_coef)
    lru_drive = jnp.sqrt(-jnp.expm1(2.0 * log_coef)) * jax.nn.sigmoid(input_pre) * conv_out
    return (lru_coef, lru_drive)

def compose(first_pair, second_pair):
    return (first_pair[0] * second_pair[0], second_pair[0] * first_pair[1] + second_pair[1])

def linear_scan(lru_coef, lru_drive):
    return lax.associative_scan(compose, (lru_coef, lru_drive), axis=0)

def feed_forward(resid, norm_gain, gate_w, up_w, down_w):
    normed = low(rms_norm(resid, norm_gain))
    gate_pre = low_back(product(normed, gate_w))
    up_pre = low_back(product(normed, up_w))
    hidden = low(low_back(gelu_tanh(gate_pre) * up_pre))
    return resid + low_back(product(hidden, down_w))

def attention_block(seq_rows, norm_gain, query_w, key_w, value_w, out_w):
    normed = low(rms_norm(seq_rows, norm_gain))
    queries = low(low_back(product(normed, query_w))).reshape(SEQ, HEADS, HEAD)
    key_rows = low(low_back(product(normed, key_w)))
    value_rows = low(low_back(product(normed, value_w)))
    padding = jnp.zeros((WINDOW, HEAD), jnp.float32)
    key_pad = jnp.concatenate([padding, key_rows], axis=0)
    value_pad = jnp.concatenate([padding, value_rows], axis=0)
    block_rows = min(SEQ, 512)
    score_scale = 1.0 / math.sqrt(HEAD)

    def one_block(block_start):
        query_blk = lax.dynamic_slice_in_dim(queries, block_start, block_rows, 0)
        key_blk = lax.dynamic_slice_in_dim(key_pad, block_start, WINDOW + block_rows, 0)
        value_blk = lax.dynamic_slice_in_dim(value_pad, block_start, WINDOW + block_rows, 0)
        raw_scores = low_back(jnp.einsum('thd,kd->htk', query_blk, key_blk, precision=HIGHEST) * score_scale)
        row_pos = block_start + jnp.arange(block_rows, dtype=jnp.int32)[:, None]
        col_pos = block_start - WINDOW + jnp.arange(WINDOW + block_rows, dtype=jnp.int32)[None, :]
        allowed = (col_pos <= row_pos) & (col_pos > row_pos - WINDOW) & (col_pos >= 0)
        scores = jnp.where(allowed[None], raw_scores, -1e+30)
        row_peak = lax.optimization_barrier(jnp.max(scores, axis=-1, keepdims=True))
        exp_scores = jnp.exp(scores - row_peak)
        attn_probs = low(exp_scores / lax.optimization_barrier(jnp.sum(exp_scores, axis=-1, keepdims=True)))
        return jnp.einsum('htk,kd->thd', attn_probs, value_blk, precision=HIGHEST)
    starts = jnp.arange(SEQ // block_rows, dtype=jnp.int32) * block_rows
    attended = lax.map(jax.checkpoint(one_block), starts).reshape(SEQ, HEADS * HEAD)
    attended = low(low_back(attended))
    return seq_rows + low_back(product(attended, out_w))

def recurrent_block(seq_rows, norm_gain, branch_w, gated_w, conv_w, rate_w, input_w, decay_w, out_w):
    normed = low(rms_norm(seq_rows, norm_gain))
    branch = low_back(product(normed, branch_w))
    gated_pre = low_back(product(normed, gated_w))
    padded = jnp.concatenate([jnp.zeros((CONV - 1, RNN), jnp.float32), branch], axis=0)
    conv_out = jnp.zeros((SEQ, RNN), jnp.float32)
    for offset in range(CONV):
        conv_out = conv_out + conv_w[:, offset] * padded[CONV - 1 - offset:CONV - 1 - offset + SEQ]
    block_width = RNN // BLOCKS
    conv_low = low(conv_out).reshape(SEQ, BLOCKS, block_width)
    rate_pre = low_back(jnp.einsum('tbi,bij->tbj', conv_low, rate_w.reshape(BLOCKS, block_width, block_width), precision=HIGHEST).reshape(SEQ, RNN))
    input_pre = low_back(jnp.einsum('tbi,bij->tbj', conv_low, input_w.reshape(BLOCKS, block_width, block_width), precision=HIGHEST).reshape(SEQ, RNN))
    lru_coef, lru_drive = lru_gates(rate_pre, input_pre, decay_w, conv_out)
    lru_state = linear_scan(lru_coef, lru_drive)[1]
    mix_out = low(low_back(lru_state * gelu_tanh(gated_pre)))
    return seq_rows + low_back(product(mix_out, out_w))

def sequence_forward(seq_rows, params):
    attn_gain, query_w, key_w, value_w, attn_w, first_gain, first_gate_w, first_up_w, first_down_w, mix_gain, branch_w, gated_w, conv_w, rate_w, input_w, decay_w, mix_w, second_gain, second_gate_w, second_up_w, second_down_w = params
    after_attn = attention_block(seq_rows, attn_gain, query_w, key_w, value_w, attn_w)
    middle = feed_forward(after_attn, first_gain, first_gate_w, first_up_w, first_down_w)
    after_mix = recurrent_block(middle, mix_gain, branch_w, gated_w, conv_w, rate_w, input_w, decay_w, mix_w)
    return feed_forward(after_mix, second_gain, second_gate_w, second_up_w, second_down_w)

def reference(tokens_in, lengths, cotangent, attn_norm, query_proj, key_proj, value_proj, attn_out, first_norm, first_gate, first_up, first_down, mixer_norm, branch_proj, gated_proj, conv_taps, rate_gate, input_gate, decay_rate, mixer_out, second_norm, second_gate, second_up, second_down):
    params = tuple((weight.astype(jnp.float32) for weight in (attn_norm, query_proj, key_proj, value_proj, attn_out, first_norm, first_gate, first_up, first_down, mixer_norm, branch_proj, gated_proj, conv_taps, rate_gate, input_gate, decay_rate, mixer_out, second_norm, second_gate, second_up, second_down)))

    def sequence_step(grad_sums, seq_item):
        seq_rows, seq_cot, length = seq_item
        result, pullback = jax.vjp(sequence_forward, seq_rows.astype(jnp.float32), params)
        valid_mask = (jnp.arange(SEQ, dtype=jnp.int32) < length).astype(jnp.float32)[:, None]
        input_back, param_grads = pullback(seq_cot.astype(jnp.float32) * valid_mask)
        grad_sums = jax.tree.map(jnp.add, grad_sums, param_grads)
        return (grad_sums, (result.astype(jnp.bfloat16), input_back.astype(jnp.bfloat16)))
    zeros_init = tuple((jnp.zeros(weight.shape, jnp.float32) for weight in params))
    totals, (outputs, input_grads) = lax.scan(sequence_step, zeros_init, (tokens_in, cotangent, lengths))
    return (outputs, input_grads, totals[0], totals[1], totals[2], totals[3], totals[4], totals[5], totals[6], totals[7], totals[8], totals[9], totals[10], totals[11], totals[12], totals[13], totals[14], totals[15], totals[16], totals[17], totals[18], totals[19], totals[20])
```

```python
import functools
import math

import jax
import jax.numpy as jnp
from jax import lax
from jax.experimental import pallas as pl
from jax.experimental.pallas import tpu as pltpu
from jax.sharding import PartitionSpec as P

WINDOW = 1024
LAG = 1
EPSILON = 1e-06
F32 = jnp.float32
BF16 = jnp.bfloat16


def rms_norm(values, norm_gain):
    return (
        values * lax.rsqrt(jnp.mean(values * values, axis=-1, keepdims=True) + EPSILON) * norm_gain
    )


def gelu_tanh(values):
    return jax.nn.gelu(values, approximate=True)


def mlp_middle(gate_pre, up_pre):
    return gelu_tanh(gate_pre) * up_pre


def lru_gates(rate_pre, input_pre, decay_w, conv_out):
    log_coef = -8.0 * jax.nn.sigmoid(rate_pre) * decay_w
    lru_coef = jnp.exp(log_coef)
    lru_drive = jnp.sqrt(-jnp.expm1(2.0 * log_coef)) * jax.nn.sigmoid(input_pre) * conv_out
    return (lru_coef, lru_drive)


def matmul(first_op, second_op):
    return jnp.dot(first_op, second_op, preferred_element_type=F32)


def matmul_left(first_op, second_op):
    return lax.dot_general(
        first_op, second_op, (((0,), (0,)), ((), ())), preferred_element_type=F32
    )


def matmul_right(first_op, second_op):
    return lax.dot_general(
        first_op, second_op, (((1,), (1,)), ((), ())), preferred_element_type=F32
    )


def rounded(values):
    return values.astype(BF16).astype(F32)


def my_chip():
    return lax.axis_index("shard") // 2


def my_core():
    return lax.rem(lax.axis_index("shard"), 2)


def swap_cores(x):
    count = lax.axis_size("shard")
    return lax.ppermute(x, "shard", [(i, i ^ 1) for i in range(count)])


def shift_rep(x, by):
    size = lax.axis_size("rep")
    return lax.ppermute(x, "rep", [(i, i + by) for i in range(size) if 0 <= i + by < size])


def shift_chip(x, by):
    count = lax.axis_size("shard")
    return lax.ppermute(x, "shard", [(i, (i + 2 * by) % count) for i in range(count)])


def by_core(first, second):
    return jnp.where(my_core() == 0, first, second)


def unit_pieces(columns, unit, parts):
    sub = unit // parts
    chips = columns // unit // 2
    return sub, tuple(
        [(2 * chip + core) * unit + part * sub for part in range(parts) for chip in range(chips)]
        for core in (0, 1)
    )


def column_halves(w, unit, parts=1):
    sub, places = unit_pieces(w.shape[1], unit, parts)
    return tuple(
        jnp.concatenate([w[:, at : at + sub] for at in places[core]], axis=1) for core in (0, 1)
    )


def joined_columns(first, second, unit, parts=1):
    sub, places = unit_pieces(2 * first.shape[1], unit, parts)
    pieces = {}
    for half, starts in zip((first, second), places):
        for i, at in enumerate(starts):
            pieces[at] = half[:, i * sub : (i + 1) * sub]
    return jnp.concatenate([pieces[at] for at in sorted(pieces)], axis=1)


def chip_rows(halves):
    own = by_core(halves[0], halves[1])
    other = swap_cores(by_core(halves[1], halves[0]))
    return jnp.concatenate([by_core(own, other), by_core(other, own)], axis=0)


def rep_masks(flip):
    size = lax.axis_size("rep")
    masks = [1 << i for i in range(size.bit_length() - 1)]
    return masks[::-1] if flip else masks


def swap_rep(x, mask):
    size = lax.axis_size("rep")
    return lax.ppermute(x, "rep", [(i, i ^ mask) for i in range(size)])


MESH_ID = pl.DeviceIdType.MESH


def across(place, mask):
    return place + mask - 2 * mask * lax.rem(place // mask, 2)


def highest(at):
    return 1 << (at.bit_length() - 1)


def lowest(at):
    return at & -at


def gather_kernel(chunks, arrays, chips, reps, *refs):
    ins, outs = refs[:arrays], refs[arrays : 2 * arrays]
    along_send, along_recv, rep_send, rep_recv, local_sem = refs[2 * arrays :]
    shard = lax.axis_index("shard")
    chip, core = shard // 2, lax.rem(shard, 2)
    place = lax.axis_index("rep")
    bits = [1 << i for i in range(reps.bit_length() - 1)]
    everyone = range(1, reps)

    def device_at(chip_at):
        return {"shard": 2 * chip_at + core}

    barrier = pltpu.get_barrier_semaphore()
    for by in (1, chips - 1):
        pl.semaphore_signal(
            barrier,
            inc=1,
            device_id=device_at(lax.rem(chip + by, chips)),
            device_id_type=MESH_ID,
        )
    for bit in bits:
        pl.semaphore_signal(
            barrier, inc=1, device_id={"rep": across(place, bit)}, device_id_type=MESH_ID
        )
    pl.semaphore_wait(barrier, 2 + len(bits))

    def block(c, rep_at, chip_at, half=None):
        array, first, columns, sub, split = chunks[c]
        row = (rep_at * chips + chip_at) * sub if split else chip_at * sub
        if half is not None:
            columns = columns // 2
            first = first + half * columns
        return outs[array].at[pl.ds(pl.multiple_of(row, 16), sub), pl.ds(first, columns)]

    def own(c):
        array, first, columns, sub, split = chunks[c]
        row = pl.multiple_of(place * sub, 16) if split else 0
        return ins[array].at[pl.ds(row, sub), pl.ds(first, columns)]

    def along(c, origin, to, direction):
        here = block(c, place, origin)
        return here, pltpu.make_async_remote_copy(
            src_ref=here,
            dst_ref=here,
            send_sem=along_send.at[c, origin, direction],
            recv_sem=along_recv.at[c, origin],
            device_id=device_at(to),
            device_id_type=MESH_ID,
        )

    def first_along(c, to, direction):
        return pltpu.make_async_remote_copy(
            src_ref=own(c),
            dst_ref=block(c, place, chip),
            send_sem=along_send.at[c, chip, direction],
            recv_sem=along_recv.at[c, chip],
            device_id=device_at(to),
            device_id_type=MESH_ID,
        )

    def hop(c, chip_at, at, half):
        bit = at if half is None else (highest(at) if half == 0 else lowest(at))
        here = block(c, across_all(place, at ^ bit), chip_at, half)
        slot = 2 * at + (half or 0)
        return pltpu.make_async_remote_copy(
            src_ref=here,
            dst_ref=here,
            send_sem=rep_send.at[c, chip_at, slot],
            recv_sem=rep_recv.at[c, chip_at, slot],
            device_id={"rep": across(place, bit)},
            device_id_type=MESH_ID,
        )

    def arrival(c, chip_at, at, half):
        here = block(c, across_all(place, at), chip_at, half)
        slot = 2 * at + (half or 0)
        return pltpu.make_async_remote_copy(
            src_ref=here,
            dst_ref=here,
            send_sem=rep_send.at[c, chip_at, slot],
            recv_sem=rep_recv.at[c, chip_at, slot],
            device_id={"rep": place},
            device_id_type=MESH_ID,
        )

    def across_all(at, offset):
        for bit in bits:
            if offset & bit:
                at = across(at, bit)
        return at

    def halves(at):
        return (None,) if at == lowest(at) else (0, 1)

    def local_copies(c):
        array, first, columns, sub, split = chunks[c]
        copies = []
        for part in range(reps if split else 1):
            copies.append(
                pltpu.make_async_copy(
                    ins[array].at[pl.ds(part * sub, sub), pl.ds(first, columns)],
                    block(c, part, chip),
                    local_sem.at[c, part],
                )
            )
        return copies

    def others(run):
        def one(by, carry):
            run(lax.rem(chip + by, chips))
            return carry

        lax.fori_loop(1, chips, one, 0)

    def begin(c):
        @pl.when(chip < chips - 1)
        def _():
            first_along(c, chip + 1, 0).start()

        @pl.when(chip > 0)
        def _():
            first_along(c, chip - 1, 1).start()

        for copy in local_copies(c):
            copy.start()

    def spread(c, origin):
        if chunks[c][4]:
            for bit in bits:
                hop(c, origin, bit, None).start()

    def arrived(c, by):
        @pl.when(chip - by >= 0)
        def _():
            along(c, chip - by, chip, 0)[1].wait_recv()

            @pl.when(chip < chips - 1)
            def _():
                along(c, chip - by, chip + 1, 0)[1].start()

            spread(c, chip - by)

        @pl.when(chip + by < chips)
        def _():
            along(c, chip + by, chip, 1)[1].wait_recv()

            @pl.when(chip > 0)
            def _():
                along(c, chip + by, chip - 1, 1)[1].start()

            spread(c, chip + by)

    def passed(c, level):
        if not chunks[c][4]:
            return

        def run(origin):
            for at in everyone:
                if at.bit_count() == level:
                    for half in halves(at):
                        arrival(c, origin, at, half).wait_recv()
            for at in everyone:
                if at.bit_count() == level + 1:
                    for half in halves(at):
                        hop(c, origin, at, half).start()

        others(run)

    def end(c):
        @pl.when(chip < chips - 1)
        def _():
            first_along(c, chip + 1, 0).wait_send()

        @pl.when(chip > 0)
        def _():
            first_along(c, chip - 1, 1).wait_send()

        for copy in local_copies(c):
            copy.wait()
        for by in range(1, chips):

            @pl.when((chip - by >= 0) & (chip < chips - 1))
            def _(by=by):
                along(c, chip - by, chip + 1, 0)[1].wait_send()

            @pl.when((chip + by < chips) & (chip > 0))
            def _(by=by):
                along(c, chip + by, chip - 1, 1)[1].wait_send()

        if chunks[c][4]:

            def run(origin):
                for at in everyone:
                    for half in halves(at):
                        hop(c, origin, at, half).wait_send()

            others(run)

    stages = (
        [begin]
        + [functools.partial(arrived, by=by) for by in range(1, chips)]
        + [functools.partial(passed, level=level) for level in range(1, len(bits) + 1)]
        + [end]
    )
    for tick in range(len(chunks) + (len(stages) - 1) * LAG):
        for at, stage in enumerate(stages):
            if 0 <= tick - at * LAG < len(chunks):
                stage(tick - at * LAG)


def gather_all(arrays, splits, widths):
    reps, chips = lax.axis_size("rep"), lax.axis_size("shard") // 2
    if any(split and array.shape[0] // reps % 16 for array, split in zip(arrays, splits)):
        results = []
        for array, split in zip(arrays, splits):
            if split:
                part = array.shape[0] // reps
                array = lax.dynamic_slice_in_dim(array, lax.axis_index("rep") * part, part, 0)
            array = lax.all_gather(
                array,
                "shard",
                axis=0,
                tiled=True,
                axis_index_groups=[list(range(core, 2 * chips, 2)) for core in (0, 1)],
            )
            results.append(lax.all_gather(array, "rep", axis=0, tiled=True) if split else array)
        return results
    chunks = []
    for i, (array, split, wide) in enumerate(zip(arrays, splits, widths)):
        sub = array.shape[0] // reps if split else array.shape[0]
        for first in range(0, array.shape[1], wide):
            chunks.append((i, first, min(wide, array.shape[1] - first), sub, split))
    slots = 2 * reps
    count = len(chunks)
    return pl.pallas_call(
        functools.partial(gather_kernel, chunks, len(arrays), chips, reps),
        in_specs=[pl.BlockSpec(memory_space=pltpu.VMEM)] * len(arrays),
        out_specs=[pl.BlockSpec(memory_space=pl.ANY)] * len(arrays),
        out_shape=[
            jax.ShapeDtypeStruct((a.shape[0] * chips, a.shape[1]), a.dtype) for a in arrays
        ],
        scratch_shapes=[
            pltpu.SemaphoreType.DMA((count, chips, 2)),
            pltpu.SemaphoreType.DMA((count, chips)),
            pltpu.SemaphoreType.DMA((count, chips, slots)),
            pltpu.SemaphoreType.DMA((count, chips, slots)),
            pltpu.SemaphoreType.DMA((count, reps)),
        ],
        compiler_params=pltpu.CompilerParams(
            collective_id=0, has_side_effects=True, vmem_limit_bytes=40 * 1024 * 1024
        ),
    )(*arrays)


def sum_chips(parts):
    chips = lax.axis_size("shard") // 2
    chip = my_chip()
    sub = parts[0].shape[0] // chips

    def rows_of(by):
        at = lax.rem(chip + by, chips) * sub
        return jnp.concatenate(
            [lax.dynamic_slice_in_dim(part, at, sub, 0) for part in parts], axis=1
        )

    total = rows_of(0).astype(F32)
    for by in range(1, chips):
        total = total + shift_chip(rows_of(by), by).astype(F32)
    return total.astype(BF16)


def sum_rep(x):
    middle = x.shape[1] // 2
    halves = [x[:, :middle], x[:, middle:]]
    for flip in (0, 1):
        for mask in rep_masks(flip):
            here = halves[flip]
            halves[flip] = (here.astype(F32) + swap_rep(here, mask).astype(F32)).astype(BF16)
    return jnp.concatenate(halves, axis=1)


def reduce_kernel(chunks, counts, chips, *refs):
    n_left, n_right, n_given, n_out = counts
    n = len(chunks)
    refs = list(refs)

    def take(count):
        taken = refs[:count]
        del refs[:count]
        return taken

    lefts, rights, givens = take(n_left), take(n_right), take(n_given)
    outs, first_in, second_in, chip_in = take(n_out), take(n), take(n), take(n)
    right_buf, big_left, first_out, first_loc, second_out, second_loc = take(6)
    chip_out, chip_loc, own_out = take(3)
    send, recv, chip_send, chip_recv, hop_send, hop_recv, local = take(7)
    shard = lax.axis_index("shard")
    chip, core = shard // 2, lax.rem(shard, 2)
    place = lax.axis_index("rep")
    bits = (1, 2)

    def device_at(chip_at):
        return {"shard": 2 * chip_at + core}

    barrier = pltpu.get_barrier_semaphore()
    for by in range(1, chips):
        pl.semaphore_signal(
            barrier,
            inc=1,
            device_id=device_at(lax.rem(chip + by, chips)),
            device_id_type=MESH_ID,
        )
    for bit in bits:
        pl.semaphore_signal(
            barrier, inc=1, device_id={"rep": across(place, bit)}, device_id_type=MESH_ID
        )
    pl.semaphore_wait(barrier, chips - 1 + len(bits))

    def rep_at(offset):
        at = place
        for bit in bits:
            if offset & bit:
                at = across(at, bit)
        return at

    def masks(c):
        return bits[::-1] if chunks[c]["flip"] else bits

    def rows_of(c):
        return chips * chunks[c]["sub"]

    def right_copy(c):
        k = chunks[c]
        return pltpu.make_async_copy(
            rights[k["right"]].at[:, pl.ds(k["first"], k["wide"])],
            right_buf.at[c % 6, :, pl.ds(0, k["wide"])],
            local.at[c, 0],
        )

    def left_copy(c):
        return pltpu.make_async_copy(lefts[chunks[c]["left"]], big_left, local.at[c, 1])

    def exchange(c, turn):
        k, rows = chunks[c], rows_of(c)
        source, target = ((first_out, first_in), (second_out, second_in))[turn]
        return pltpu.make_async_remote_copy(
            src_ref=source.at[c % 3, :, pl.ds(0, rows), pl.ds(0, k["wide"])],
            dst_ref=target[c],
            send_sem=send.at[c, turn],
            recv_sem=recv.at[c, turn],
            device_id={"rep": across(place, masks(c)[turn])},
            device_id_type=MESH_ID,
        )

    def arrived_copy(c, turn):
        k, rows = chunks[c], rows_of(c)
        source = (first_in, second_in)[turn][c]
        target = (first_loc.at[c % 4], second_loc.at[c % 2])[turn]
        return pltpu.make_async_copy(
            source, target.at[:, pl.ds(0, rows), pl.ds(0, k["wide"])], local.at[c, 2 + turn]
        )

    def tiles(c, run):
        wide = chunks[c]["wide"]
        tile = 256 if wide % 256 == 0 else 128

        def one(i, carry):
            run(pl.ds(pl.multiple_of(i * tile, tile), tile))
            return carry

        lax.fori_loop(0, wide // tile, one, 0)

    def product(c, offset, target, arrivals):
        k, rows = chunks[c], rows_of(c)
        at = rep_at(offset)

        def run(columns):
            if k["given"] is not None:
                total = givens[k["given"]][at, :, columns].astype(F32)
            else:
                left = big_left if k["big"] else lefts[k["left"]]
                total = jnp.dot(
                    left[at], right_buf[c % 6, :, columns], preferred_element_type=F32
                )
            for ref, index in arrivals:
                total = total + ref[index + (pl.ds(0, rows), columns)].astype(F32)
            target[0][target[1] + (pl.ds(0, rows), columns)] = total.astype(BF16)

        tiles(c, run)

    def load(c):
        if chunks[c]["given"] is None:
            right_copy(c).start()
            if chunks[c]["load"]:
                left_copy(c).start()

    def send_first(c):
        if chunks[c]["given"] is None:
            right_copy(c).wait()
            if chunks[c]["load"]:
                left_copy(c).wait()
        one, two = masks(c)
        product(c, one, (first_out, (c % 3, 0)), [])
        product(c, one ^ two, (first_out, (c % 3, 1)), [])
        exchange(c, 0).start()

    def take_first(c):
        exchange(c, 0).wait_recv()
        arrived_copy(c, 0).start()

    def send_second(c):
        arrived_copy(c, 0).wait()
        product(c, masks(c)[1], (second_out, (c % 3, 0)), [(first_loc, (c % 4, 1))])
        exchange(c, 1).start()
        exchange(c, 0).wait_send()

    def take_second(c):
        exchange(c, 1).wait_recv()
        arrived_copy(c, 1).start()

    def to_chip(c, by):
        k = chunks[c]
        at = lax.rem(chip + by, chips)
        row = pl.multiple_of(at * k["sub"], 16)
        return pltpu.make_async_remote_copy(
            src_ref=chip_out.at[c % 3, pl.ds(row, k["sub"]), pl.ds(0, k["wide"])],
            dst_ref=chip_in[c].at[by - 1],
            send_sem=chip_send.at[c, by - 1],
            recv_sem=chip_recv.at[c, by - 1],
            device_id=device_at(at),
            device_id_type=MESH_ID,
        )

    def send_chips(c):
        arrived_copy(c, 1).wait()
        product(
            c, 0, (chip_out, (c % 3,)), [(first_loc, (c % 4, 0)), (second_loc, (c % 2, 0))]
        )
        for by in range(1, chips):
            to_chip(c, by).start()
        exchange(c, 1).wait_send()

    def chips_copy(c):
        k = chunks[c]
        return pltpu.make_async_copy(
            chip_in[c],
            chip_loc.at[c % 2, :, pl.ds(0, k["sub"]), pl.ds(0, k["wide"])],
            local.at[c, 4],
        )

    def take_chips(c):
        for by in range(1, chips):
            to_chip(c, by).wait_recv()
        chips_copy(c).start()

    def out_rows(c, offset, half=None):
        k = chunks[c]
        first, wide = k["place"], k["wide"]
        if half is not None:
            wide = wide // 2
            first = first + half * wide
        row = pl.multiple_of(rep_at(offset) * k["sub"], 16)
        return outs[k["out"]].at[pl.ds(row, k["sub"]), pl.ds(first, wide)]

    def own_rows_of(c):
        k = chunks[c]
        return own_out.at[c % 3, pl.ds(0, k["sub"]), pl.ds(0, k["wide"])]

    def own_copy(c):
        return pltpu.make_async_copy(own_rows_of(c), out_rows(c, 0), local.at[c, 5])

    def hop(c, at, half):
        bit = at if at in bits else (2 if half != 1 else 1)
        here = out_rows(c, at ^ bit, half)
        slot = 2 * at + (half or 0)
        return pltpu.make_async_remote_copy(
            src_ref=own_rows_of(c) if at in bits else here,
            dst_ref=here,
            send_sem=hop_send.at[c, slot],
            recv_sem=hop_recv.at[c, slot],
            device_id={"rep": across(place, bit)},
            device_id_type=MESH_ID,
        )

    def arrival(c, at, half):
        here = out_rows(c, at, half)
        slot = 2 * at + (half or 0)
        return pltpu.make_async_remote_copy(
            src_ref=here,
            dst_ref=here,
            send_sem=hop_send.at[c, slot],
            recv_sem=hop_recv.at[c, slot],
            device_id={"rep": across(place, 1)},
            device_id_type=MESH_ID,
        )

    def far_halves(c):
        return (0, 1) if chunks[c]["wide"] % 256 == 0 else (None,)

    def send_sums(c):
        k = chunks[c]
        chips_copy(c).wait()
        row = pl.multiple_of(chip * k["sub"], 16)

        def run(columns):
            total = chip_out[c % 3, pl.ds(row, k["sub"]), columns].astype(F32)
            for by in range(1, chips):
                total = total + chip_loc[c % 2, by - 1, pl.ds(0, k["sub"]), columns].astype(F32)
            own_out[c % 3, pl.ds(0, k["sub"]), columns] = total.astype(BF16)

        tiles(c, run)
        for bit in bits:
            hop(c, bit, None).start()
        own_copy(c).start()
        for by in range(1, chips):
            to_chip(c, by).wait_send()

    def pass_sums(c):
        for bit in bits:
            arrival(c, bit, None).wait_recv()
        for half in far_halves(c):
            hop(c, 3, half).start()

    def end(c):
        own_copy(c).wait()
        for bit in bits:
            hop(c, bit, None).wait_send()
        for half in far_halves(c):
            arrival(c, 3, half).wait_recv()
            hop(c, 3, half).wait_send()

    stages = [
        load,
        send_first,
        take_first,
        send_second,
        take_second,
        send_chips,
        take_chips,
        send_sums,
        pass_sums,
        end,
    ]
    for tick in range(n + len(stages) - 1):
        for at, stage in enumerate(stages):
            if 0 <= tick - at < n:
                stage(tick - at)


def reduce_all(products):
    reps, chips = lax.axis_size("rep"), lax.axis_size("shard") // 2
    depth = max(left.shape[0] for left, _, _ in products if left is not None)
    if reps != 4 or any(
        (given[0].shape[1] if left is None else left.shape[1] // reps) // chips % 16
        for left, given, _ in products
    ):
        results = []
        for left, given, _ in products:
            if left is None:
                whole = given[0].reshape(-1, given[0].shape[2])
            else:
                whole = jnp.concatenate(
                    [matmul_left(left, right).astype(BF16) for right in given], axis=1
                )
            part = lax.psum_scatter(whole, "rep", scatter_dimension=0, tiled=True)
            count = lax.axis_size("shard")
            part = lax.psum_scatter(
                part,
                "shard",
                scatter_dimension=0,
                tiled=True,
                axis_index_groups=[list(range(core, count, 2)) for core in (0, 1)],
            )
            results.append(lax.all_gather(part, "rep", axis=0, tiled=True))
        return results
    lefts, rights, givens, chunks, outs = [], [], [], [], []
    subs = [
        (given[0].shape[1] if left is None else left.shape[1] // reps) // chips
        for left, given, _ in products
    ]
    small = min(subs)
    for (left, parts, wide), sub in zip(products, subs):
        total = sum(part.shape[-1] for part in parts)
        outs.append(jax.ShapeDtypeStruct((reps * sub, total), BF16))
        first_right = len(rights)
        if left is not None:
            lefts.append(left.T.reshape(reps, chips * sub, depth))
            rights.extend(parts)
        else:
            givens.extend(parts)
        before = 0
        mine = []
        for i, part in enumerate(parts):
            row = []
            for first in range(0, part.shape[-1], wide):
                row.append(
                    dict(
                        left=len(lefts) - 1,
                        given=len(givens) - 1 if left is None else None,
                        right=first_right + i,
                        first=first,
                        wide=min(wide, part.shape[-1] - first),
                        sub=sub,
                        out=len(outs) - 1,
                        place=before + first,
                        big=sub > small,
                        load=False,
                    )
                )
            mine.append(row)
            before += part.shape[-1]
        mine = [chunk for group in zip(*mine) for chunk in group]
        mine[0]["load"] = sub > small
        chunks += mine
    for i, chunk in enumerate(chunks):
        chunk["flip"] = i % 2
    n = len(chunks)
    rows = max(subs) * chips
    wide = max(chunk["wide"] for chunk in chunks)
    hbm = pl.BlockSpec(memory_space=pl.ANY)
    vmem = pl.BlockSpec(memory_space=pltpu.VMEM)
    big = {chunk["left"] for chunk in chunks if chunk["big"]}

    def landing(blocks, sub_only=False):
        return [
            jax.ShapeDtypeStruct(
                (blocks, c["sub"] if sub_only else chips * c["sub"], c["wide"]), BF16
            )
            for c in chunks
        ]

    shapes = outs + landing(2) + landing(1) + landing(chips - 1, True)
    results = pl.pallas_call(
        functools.partial(
            reduce_kernel, chunks, (len(lefts), len(rights), len(givens), len(outs)), chips
        ),
        in_specs=[hbm if i in big else vmem for i in range(len(lefts))]
        + [hbm] * len(rights)
        + [vmem] * len(givens),
        out_specs=[hbm] * len(shapes),
        out_shape=shapes,
        scratch_shapes=[
            pltpu.VMEM((6, depth, wide), BF16),
            pltpu.VMEM((reps, rows, depth), BF16),
            pltpu.VMEM((3, 2, rows, wide), BF16),
            pltpu.VMEM((4, 2, rows, wide), BF16),
            pltpu.VMEM((3, 1, rows, wide), BF16),
            pltpu.VMEM((2, 1, rows, wide), BF16),
            pltpu.VMEM((3, rows, wide), BF16),
            pltpu.VMEM((2, chips - 1, max(subs), wide), BF16),
            pltpu.VMEM((3, max(subs), wide), BF16),
            pltpu.SemaphoreType.DMA((n, 2)),
            pltpu.SemaphoreType.DMA((n, 2)),
            pltpu.SemaphoreType.DMA((n, chips - 1)),
            pltpu.SemaphoreType.DMA((n, chips - 1)),
            pltpu.SemaphoreType.DMA((n, 8)),
            pltpu.SemaphoreType.DMA((n, 8)),
            pltpu.SemaphoreType.DMA((n, 6)),
        ],
        compiler_params=pltpu.CompilerParams(
            collective_id=1, has_side_effects=True, vmem_limit_bytes=62 * 1024 * 1024
        ),
    )(*lefts, *rights, *givens)
    return results[: len(outs)]


def reduce_chips(grads):
    return sum_rep(sum_chips(grads))


def own_rows(rows):
    part = rows.shape[0] // 2
    first, second = rows[:part], rows[part:]
    keep = by_core(first, second)
    got = swap_cores(by_core(second, first))
    return by_core(keep, got), by_core(got, keep)


def scan_kernel(reverse, coef_ref, drive_ref, cum_ref, out_ref):
    rows, lanes = coef_ref.shape[1], coef_ref.shape[2]
    groups = rows // 8
    place = lax.broadcasted_iota(jnp.int32, (8, lanes), 0)

    def step(turn, carry):
        carry_cum, carry_out = carry
        group = groups - 1 - turn if reverse else turn
        where = pl.ds(pl.multiple_of(group * 8, 8), 8)
        a = coef_ref[0, where, :]
        b = drive_ref[0, where, :]
        for k in (1, 2, 4):
            by = 8 - k if reverse else k
            inside = place < 8 - k if reverse else place >= k
            a_before = jnp.where(inside, pltpu.roll(a, by, 0), 1.0)
            b_before = jnp.where(inside, pltpu.roll(b, by, 0), 0.0)
            b = a * b_before + b
            a = a * a_before
        out = b + a * carry_out
        cum = a * carry_cum
        out_ref[0, where, :] = out
        cum_ref[0, where, :] = cum
        last = 0 if reverse else 7
        return (
            jnp.broadcast_to(cum[last : last + 1], (8, lanes)),
            jnp.broadcast_to(out[last : last + 1], (8, lanes)),
        )

    lax.fori_loop(
        0, groups, step, (jnp.ones((8, lanes), F32), jnp.zeros((8, lanes), F32))
    )


def linear_scan(coef, drive, reverse):
    batch, rows, width = coef.shape
    lanes = min(512, width)
    spec = pl.BlockSpec((1, rows, lanes), lambda b, i: (b, 0, i))
    shape = jax.ShapeDtypeStruct(coef.shape, F32)
    return pl.pallas_call(
        functools.partial(scan_kernel, reverse),
        grid=(batch, width // lanes),
        in_specs=[spec, spec],
        out_specs=[spec, spec],
        out_shape=[shape, shape],
        compiler_params=pltpu.CompilerParams(vmem_limit_bytes=48 * 1024 * 1024),
    )(coef, drive)


def carried_in(prod, part, reverse):
    size = lax.axis_size("rep")
    pair = jnp.stack([prod, part])
    total = jnp.zeros_like(part)
    through = jnp.ones_like(prod)
    place = lax.axis_index("rep")
    ahead = size - 1 - place if reverse else place
    for distance in range(1, size):
        got = shift_rep(pair, -distance if reverse else distance)
        total = total + through * got[1]
        through = jnp.where(ahead >= distance, through * got[0], through)
    return total


def window_scores(query_heads, key_win, start_row, behind):
    row_count = query_heads.shape[0]
    score_scale = 1.0 / math.sqrt(query_heads.shape[2])
    raw_scores = (
        jnp.einsum("thd,kd->htk", query_heads, key_win, preferred_element_type=F32) * score_scale
    )
    row_pos = start_row + jnp.arange(row_count, dtype=jnp.int32)[:, None]
    col_pos = start_row - behind + jnp.arange(key_win.shape[0], dtype=jnp.int32)[None, :]
    allowed = (col_pos <= row_pos) & (col_pos > row_pos - WINDOW) & (col_pos >= 0)
    return jnp.where(allowed[None], raw_scores, -1e30)


def with_sibling(x):
    return jnp.concatenate([x, swap_cores(x)], axis=0)


def sum_parts(parts):
    rows = parts.shape[0] // 2
    return parts[:rows] + swap_cores(parts[rows:])


def mlp_forward(resid, norm_gain, in_w, down_w):
    normed = with_sibling(rms_norm(resid, norm_gain).astype(BF16))
    middle = in_w.shape[1] // 2
    both = matmul(normed, in_w)
    gate_pre, up_pre = both[:, :middle], both[:, middle:]
    hidden = mlp_middle(gate_pre, up_pre).astype(BF16)
    return resid + sum_parts(matmul(hidden, down_w)), (normed, gate_pre, up_pre, hidden)


def mlp_backward(resid, norm_gain, in_w, down_w, kept_vals, back_out):
    normed, gate_pre, up_pre, hidden = kept_vals
    out_low = with_sibling(back_out.astype(BF16))
    back_hidden = rounded(matmul_right(out_low, down_w))
    back_gate, back_up = jax.vjp(mlp_middle, gate_pre, up_pre)[1](back_hidden)
    gate_low = back_gate.astype(BF16)
    up_low = back_up.astype(BF16)
    back_normed = sum_parts(matmul_right(jnp.concatenate([gate_low, up_low], axis=1), in_w))
    back_resid, grad_gain = jax.vjp(rms_norm, resid, norm_gain)[1](back_normed)
    return (back_out + back_resid, (grad_gain, (normed, gate_low), (normed, up_low), (hidden, out_low)))


def on_device(
    tokens_in,
    lengths,
    cotangent,
    attn_norm,
    query_proj,
    key_proj,
    value_proj,
    attn_out,
    first_norm,
    first_gate,
    first_up,
    first_down,
    mixer_norm,
    branch_proj,
    gated_proj,
    conv_taps,
    rate_gate,
    input_gate,
    decay_rate,
    mixer_out,
    second_norm,
    second_gate,
    second_up,
    second_down,
):
    row_count = tokens_in.shape[1]
    width = tokens_in.shape[2]
    shards = lax.axis_size("shard")
    reps = lax.axis_size("rep")
    chips = shards // 2
    core = my_core()
    start_row = lax.axis_index("rep") * row_count
    positions = start_row + jnp.arange(row_count, dtype=jnp.int32)
    valid_mask = (positions < lengths[0]).astype(F32)[:, None]

    piece = width // chips // reps
    spot = lax.broadcasted_iota(jnp.int32, (width, width), 1)
    natural = (
        lax.rem(spot // piece, chips) * (piece * reps)
        + (spot // (piece * chips)) * piece
        + lax.rem(spot, piece)
    )
    to_order = (lax.broadcasted_iota(jnp.int32, (width, width), 0) == natural).astype(BF16)

    def ordered(x):
        return matmul(x, to_order)

    def unordered(x):
        return matmul_right(x, to_order)

    head_size = key_proj.shape[1]
    half = query_proj.shape[1] // 2
    gain_columns = jnp.stack([attn_norm, first_norm, mixer_norm, second_norm], axis=1)
    gain_columns = jnp.pad(gain_columns, ((0, 0), (0, 128 - 4)))
    qkv_halves = (
        jnp.concatenate([query_proj[:, :half], key_proj, gain_columns], axis=1),
        jnp.concatenate([query_proj[:, half:], value_proj, gain_columns], axis=1),
    )
    out_ordered = ordered(attn_out).astype(BF16)
    out_halves = out_ordered[:, : width // 2], out_ordered[:, width // 2 :]
    qkv_width = half + head_size
    ff_unit = first_down.shape[0]
    lru_unit = mixer_out.shape[0]

    def both_halves(first, second, unit, parts):
        pairs = zip(column_halves(first, unit, parts), column_halves(second, unit, parts))
        return tuple(jnp.concatenate(pair, axis=1) for pair in pairs)

    block_width = rate_gate.shape[1]
    tap_count = conv_taps.shape[1]
    spare = block_width - tap_count - 1
    attn_wide, first_in_w, first_down_w, lru_in_w, mix_wide, second_in_w, second_down_w = gather_all(
        (
            chip_rows(tuple(jnp.concatenate(both, axis=1) for both in zip(qkv_halves, out_halves))),
            chip_rows(both_halves(first_gate, first_up, ff_unit, reps)),
            ordered(first_down).astype(BF16),
            chip_rows(both_halves(branch_proj, gated_proj, lru_unit, 1)),
            jnp.concatenate(
                [
                    rate_gate,
                    input_gate,
                    conv_taps,
                    decay_rate[:, None],
                    jnp.zeros((lru_unit, spare), BF16),
                    ordered(mixer_out).astype(BF16),
                ],
                axis=1,
            ),
            chip_rows(both_halves(second_gate, second_up, ff_unit, reps)),
            ordered(second_down).astype(BF16),
        ),
        (True, True, True, True, False, True, True),
        (1792, 1536, 1536, 1024, 1920, 1536, 1536),
    )
    qkv_own = attn_wide[:, :qkv_width]
    gains = attn_wide[:, qkv_width : qkv_width + 128].astype(F32)
    gain_attn, gain_first, gain_mix, gain_second = (gains[:, i] for i in range(4))
    attn_own = attn_wide[:, qkv_width + 128 :]
    qkv_sib = swap_cores(qkv_own)
    attn_sib = swap_cores(attn_own)

    small_w = mix_wide[:, : 3 * block_width]
    mix_w = mix_wide[:, 3 * block_width :]

    inputs = ordered(tokens_in.reshape(row_count, width))
    attn_normed = rms_norm(inputs, gain_attn).astype(BF16)
    qkv_mine = matmul(attn_normed, qkv_own).astype(BF16)
    qkv_other = matmul(attn_normed, qkv_sib).astype(BF16)
    qkv_first, qkv_second = by_core(qkv_mine, qkv_other), by_core(qkv_other, qkv_mine)
    query_rows = jnp.concatenate([qkv_first[:, :half], qkv_second[:, :half]], axis=1)
    kv_rows = jnp.concatenate([qkv_first[:, half:], qkv_second[:, half:]], axis=1)
    blocks_behind = -(-WINDOW // row_count)
    behind = blocks_behind * row_count
    kv_win = jnp.concatenate(
        [shift_rep(kv_rows, by) for by in range(blocks_behind, 0, -1) if by < reps]
        + [kv_rows],
        axis=0,
    )
    behind = kv_win.shape[0] - row_count
    key_win, value_win = kv_win[:, :head_size], kv_win[:, head_size:]
    head_count = query_rows.shape[1] // head_size
    query_heads = query_rows.reshape(row_count, head_count, head_size)
    scores = window_scores(query_heads, key_win, start_row, behind)
    row_peak = jnp.max(scores, axis=-1, keepdims=True)
    exp_scores = jnp.exp(scores - row_peak)
    exp_total = jnp.sum(exp_scores, axis=-1, keepdims=True)
    log_total = row_peak + jnp.log(exp_total)
    probs_low = (exp_scores / exp_total).astype(BF16)
    attended = jnp.einsum("htk,kd->thd", probs_low, value_win, preferred_element_type=F32)
    attended_low = ordered(attended.reshape(row_count, width).astype(BF16)).astype(BF16)
    out_mine = matmul(attended_low, attn_own)
    out_other = matmul(attended_low, attn_sib)
    resid_one = inputs + jnp.concatenate(
        [by_core(out_mine, out_other), by_core(out_other, out_mine)], axis=1
    )

    middle, first_kept = mlp_forward(resid_one, gain_first, first_in_w, first_down_w)

    rate_blocks = small_w[:, :block_width].reshape(-1, block_width, block_width)
    input_blocks = small_w[:, block_width : 2 * block_width].reshape(-1, block_width, block_width)
    conv_w = small_w[:, 2 * block_width : 2 * block_width + tap_count].astype(F32)
    decay_w = small_w[:, 2 * block_width + tap_count].astype(F32)
    mix_normed = with_sibling(rms_norm(middle, gain_mix).astype(BF16))
    lru_width = lru_in_w.shape[1] // 2
    block_count = lru_width // block_width
    branch_gated = matmul(mix_normed, lru_in_w).reshape(2, row_count, 2 * lru_width)
    branch, gated_pre = branch_gated[:, :, :lru_width], branch_gated[:, :, lru_width:]
    tail_rows = shift_rep(branch[:, row_count - (tap_count - 1) :], 1)
    extended = jnp.concatenate([tail_rows, branch], axis=1)

    def earlier(offset):
        return extended[:, tap_count - 1 - offset : tap_count - 1 - offset + row_count]

    conv_out = sum(conv_w[:, offset] * earlier(offset) for offset in range(tap_count))
    conv_low = conv_out.astype(BF16).reshape(2 * row_count, block_count, block_width)

    def through_blocks(values, blocks, how):
        return jnp.einsum(how, values, blocks, preferred_element_type=F32)

    rate_pre = through_blocks(conv_low, rate_blocks, "tbi,bij->tbj").reshape(branch.shape)
    input_pre = through_blocks(conv_low, input_blocks, "tbi,bij->tbj").reshape(branch.shape)
    lru_coef, lru_drive = lru_gates(rate_pre, input_pre, decay_w, conv_out)
    cum_coef, local_state = linear_scan(lru_coef, lru_drive, False)
    start_state = carried_in(cum_coef[:, -1], local_state[:, -1], False)
    lru_state = local_state + cum_coef * start_state[:, None]
    gated_act = gelu_tanh(gated_pre)
    mix_low = (lru_state * gated_act).astype(BF16).reshape(2 * row_count, lru_width)
    resid_two = middle + sum_parts(matmul(mix_low, mix_w))

    final_rows, second_kept = mlp_forward(
        resid_two, gain_second, second_in_w, second_down_w
    )
    out_tokens = unordered(final_rows.astype(BF16)).astype(BF16).reshape(1, row_count, width)
    back_final = ordered(cotangent.reshape(row_count, width)) * valid_mask
    back_two, second_grads = mlp_backward(
        resid_two,
        gain_second,
        second_in_w,
        second_down_w,
        second_kept,
        back_final,
    )

    mix_back_low = with_sibling(back_two.astype(BF16))
    grad_mix_out = matmul_left(mix_low, mix_back_low).astype(BF16)
    back_mixed = rounded(matmul_right(mix_back_low, mix_w)).reshape(branch.shape)
    back_state = back_mixed * gated_act
    gelu_pull = jax.vjp(gelu_tanh, gated_pre)[1]
    gated_back_low = (
        gelu_pull(back_mixed * lru_state)[0].astype(BF16).reshape(2 * row_count, lru_width)
    )
    coef_next = jnp.concatenate([lru_coef[:, 1:], jnp.ones_like(lru_coef[:, :1])], axis=1)
    later_prod, local_adjoint = linear_scan(coef_next, back_state, True)
    carry_in = carried_in(cum_coef[:, -1], lru_coef[:, 0] * local_adjoint[:, 0], True)
    adjoint = local_adjoint + later_prod * carry_in[:, None]
    prev_state = jnp.concatenate([start_state[:, None], lru_state[:, :-1]], axis=1)
    gates_pull = jax.vjp(lru_gates, rate_pre, input_pre, decay_w, conv_out)[1]
    back_rate, back_input, grad_decay, back_conv_direct = gates_pull(
        (adjoint * prev_state, adjoint)
    )
    rate_back_low = back_rate.astype(BF16).reshape(conv_low.shape)
    input_back_low = back_input.astype(BF16).reshape(conv_low.shape)
    grad_rate = through_blocks(conv_low, rate_back_low, "tbi,tbj->bij")
    grad_input = through_blocks(conv_low, input_back_low, "tbi,tbj->bij")
    gate_back_conv = through_blocks(rate_back_low, rate_blocks, "tbj,bij->tbi") + through_blocks(
        input_back_low, input_blocks, "tbj,bij->tbi"
    )
    back_conv = back_conv_direct + gate_back_conv.reshape(branch.shape)
    grad_taps = jnp.stack(
        [jnp.sum(back_conv * earlier(offset), axis=(0, 1)) for offset in range(tap_count)], axis=1
    )
    next_rows = shift_rep(back_conv[:, : tap_count - 1], -1)
    back_extended = jnp.concatenate([back_conv, next_rows], axis=1)
    branch_back_low = (
        sum(
            conv_w[:, offset] * back_extended[:, offset : offset + row_count]
            for offset in range(tap_count)
        )
        .astype(BF16)
        .reshape(2 * row_count, lru_width)
    )
    back_mix_normed = sum_parts(
        matmul_right(jnp.concatenate([branch_back_low, gated_back_low], axis=1), lru_in_w)
    )
    back_middle_norm, grad_mix_gain = jax.vjp(rms_norm, middle, gain_mix)[1](back_mix_normed)
    back_middle = back_two + back_middle_norm
    grad_small = jnp.concatenate(
        [
            grad_rate.reshape(lru_width, block_width).astype(BF16),
            grad_input.reshape(lru_width, block_width).astype(BF16),
            grad_taps.astype(BF16),
            grad_decay[:, None].astype(BF16),
            jnp.zeros((lru_width, spare), BF16),
        ],
        axis=1,
    )

    back_one, first_grads = mlp_backward(
        resid_one, gain_first, first_in_w, first_down_w, first_kept, back_middle
    )

    attn_back_low = back_one.astype(BF16)
    back_halves = attn_back_low[:, : width // 2], attn_back_low[:, width // 2 :]
    back_mine, back_other = by_core(*back_halves), by_core(back_halves[1], back_halves[0])
    attended_both = with_sibling(attended_low)
    out_right = jnp.concatenate([back_mine, swap_cores(back_other)], axis=0)
    back_attended = matmul_right(back_mine, attn_own) + matmul_right(back_other, attn_sib)
    back_attended = (
        unordered(back_attended.astype(BF16))
        .astype(BF16)
        .reshape(row_count, head_count, head_size)
    )
    attn_probs = jnp.exp(window_scores(query_heads, key_win, start_row, behind) - log_total)
    probs_again = attn_probs.astype(BF16)
    back_probs = jnp.einsum("thd,kd->htk", back_attended, value_win, preferred_element_type=F32)
    prob_dot = jnp.sum(attn_probs * back_probs, axis=-1, keepdims=True)
    scores_back_low = (attn_probs * (back_probs - prob_dot)).astype(BF16)
    score_scale = 1.0 / math.sqrt(head_size)
    back_query = (
        jnp.einsum("htk,kd->thd", scores_back_low, key_win, preferred_element_type=F32)
        * score_scale
    )
    back_key_win = (
        jnp.einsum("htk,thd->kd", scores_back_low, query_heads, preferred_element_type=F32)
        * score_scale
    )
    back_value_win = jnp.einsum(
        "htk,thd->kd", probs_again, back_attended, preferred_element_type=F32
    )
    back_kv_win = jnp.concatenate([back_key_win, back_value_win], axis=1)
    back_kv = back_kv_win[behind:]
    for by in range(1, behind // row_count + 1):
        begin = behind - by * row_count
        back_kv = back_kv + shift_rep(back_kv_win[begin : begin + row_count], -by)
    back_kv = back_kv.astype(BF16)
    back_query = back_query.reshape(row_count, width).astype(BF16)
    back_first = jnp.concatenate([back_query[:, :half], back_kv[:, :head_size]], axis=1)
    back_second = jnp.concatenate([back_query[:, half:], back_kv[:, head_size:]], axis=1)
    qkv_back_mine = by_core(back_first, back_second)
    qkv_back_other = by_core(back_second, back_first)
    back_attn_normed = matmul_right(qkv_back_mine, qkv_own) + matmul_right(qkv_back_other, qkv_sib)
    back_inputs_norm, grad_attn_gain = jax.vjp(rms_norm, inputs, gain_attn)[1](back_attn_normed)
    input_grad = (
        unordered((back_one + back_inputs_norm).astype(BF16))
        .astype(BF16)
        .reshape(1, row_count, width)
    )

    mix_reduced = reduce_chips([grad_small, grad_mix_out])
    grad_mixer_out = unordered(mix_reduced[:, 3 * block_width :])
    small = mix_reduced[:, : 3 * block_width].astype(F32)

    gain_given = jnp.stack([grad_attn_gain, first_grads[0], grad_mix_gain, second_grads[0]])
    gain_given = jnp.pad(gain_given, ((0, 124), (0, 0))).astype(BF16).T.reshape(reps, -1, 128)
    qkv_right = jnp.concatenate([qkv_back_mine, swap_cores(qkv_back_other)], axis=0)
    second_in, second_down_rows, lru_in, first_in, first_down_rows, qkv_rows, out_rows, gain_rows = (
        reduce_all(
            [
                (second_grads[1][0], [second_grads[1][1], second_grads[2][1]], 768),
                (second_grads[3][0], [second_grads[3][1]], 512),
                (mix_normed, [branch_back_low, gated_back_low], 512),
                (first_grads[1][0], [first_grads[1][1], first_grads[2][1]], 768),
                (first_grads[3][0], [first_grads[3][1]], 512),
                (with_sibling(attn_normed), [qkv_right], 512),
                (with_sibling(attended_low), [out_right], 768),
                (None, [gain_given], 128),
            ]
        )
    )

    def in_reduced(reduced, unit, parts):
        rows = own_rows(reduced)
        middle = rows[0].shape[1] // 2
        return tuple(
            joined_columns(*(half[:, columns] for half in rows), unit, parts).astype(F32)
            for columns in (slice(0, middle), slice(middle, None))
        )

    grad_second_gate, grad_second_up = in_reduced(second_in, ff_unit, reps)
    grad_second_down = unordered(second_down_rows)
    grad_branch_proj, grad_gated_proj = in_reduced(lru_in, lru_unit, 1)
    grad_first_gate, grad_first_up = in_reduced(first_in, ff_unit, reps)
    grad_first_down = unordered(first_down_rows)
    qkv_first, qkv_second = own_rows(qkv_rows)
    grad_query = jnp.concatenate([qkv_first[:, :half], qkv_second[:, :half]], axis=1).astype(F32)
    grad_key = qkv_first[:, half:].astype(F32)
    grad_value = qkv_second[:, half:].astype(F32)
    grad_out_proj = unordered(jnp.concatenate(own_rows(out_rows), axis=1))
    gain_first_, gain_second_ = own_rows(gain_rows)
    gain_grads = (gain_first_.astype(F32) + gain_second_.astype(F32)).T
    return (
        out_tokens,
        input_grad,
        gain_grads[0],
        grad_query,
        grad_key,
        grad_value,
        grad_out_proj,
        gain_grads[1],
        grad_first_gate,
        grad_first_up,
        grad_first_down,
        gain_grads[2],
        grad_branch_proj,
        grad_gated_proj,
        small[:, 2 * block_width : 2 * block_width + tap_count],
        small[:, :block_width],
        small[:, block_width : 2 * block_width],
        small[:, 2 * block_width + tap_count],
        grad_mixer_out,
        gain_grads[3],
        grad_second_gate,
        grad_second_up,
        grad_second_down,
    )


def solution(mesh):
    rows = P("shard", None)
    vector = P("shard")
    tokens = P("shard", "rep", None)
    weights = (
        vector,
        rows,
        rows,
        rows,
        rows,
        vector,
        rows,
        rows,
        rows,
        vector,
        rows,
        rows,
        rows,
        rows,
        rows,
        vector,
        rows,
        vector,
        rows,
        rows,
        rows,
    )
    return jax.shard_map(
        on_device,
        mesh=mesh,
        in_specs=(tokens, vector, tokens) + weights,
        out_specs=(tokens, tokens) + weights,
        check_vma=False,
    )
```

```python
import functools
import math

import jax
import jax.numpy as jnp
from jax import lax
from jax.experimental import pallas as pl
from jax.experimental.pallas import tpu as pltpu
from jax.sharding import PartitionSpec as P

WINDOW = 1024
LAG = 1
EPSILON = 1e-06
F32 = jnp.float32
BF16 = jnp.bfloat16


def rms_norm(values, norm_gain):
    return (
        values * lax.rsqrt(jnp.mean(values * values, axis=-1, keepdims=True) + EPSILON) * norm_gain
    )


def gelu_tanh(values):
    return jax.nn.gelu(values, approximate=True)


def mlp_middle(gate_pre, up_pre):
    return gelu_tanh(gate_pre) * up_pre


def matmul(first_op, second_op):
    return jnp.dot(first_op, second_op, preferred_element_type=F32)


def matmul_left(first_op, second_op):
    return lax.dot_general(
        first_op, second_op, (((0,), (0,)), ((), ())), preferred_element_type=F32
    )


def matmul_right(first_op, second_op):
    return lax.dot_general(
        first_op, second_op, (((1,), (1,)), ((), ())), preferred_element_type=F32
    )


def rounded(values):
    return values.astype(BF16).astype(F32)


def my_chip():
    return lax.axis_index("shard") // 2


def my_core():
    return lax.rem(lax.axis_index("shard"), 2)


def swap_cores(x):
    count = lax.axis_size("shard")
    return lax.ppermute(x, "shard", [(i, i ^ 1) for i in range(count)])


def shift_rep(x, by):
    size = lax.axis_size("rep")
    return lax.ppermute(x, "rep", [(i, i + by) for i in range(size) if 0 <= i + by < size])


def shift_chip(x, by):
    count = lax.axis_size("shard")
    return lax.ppermute(x, "shard", [(i, (i + 2 * by) % count) for i in range(count)])


def by_core(first, second):
    return jnp.where(my_core() == 0, first, second)


def unit_pieces(columns, unit, parts):
    sub = unit // parts
    chips = columns // unit // 2
    return sub, tuple(
        [(2 * chip + core) * unit + part * sub for part in range(parts) for chip in range(chips)]
        for core in (0, 1)
    )


def split_kernel(sub, places, core_ref, *refs):
    ins, (mine, other) = refs[:-2], refs[-2:]

    def run(core):
        for k, out in ((core, mine), (1 - core, other)):
            column = 0
            for ref in ins:
                for at in places[k]:
                    out[:, column : column + sub] = ref[:, at : at + sub]
                    column += sub

    for core in (0, 1):
        pl.when(core_ref[0] == core)(functools.partial(run, core))


def split_columns(arrays, unit, parts=1):
    sub, places = unit_pieces(arrays[0].shape[1], unit, parts)
    rows, width = arrays[0].shape
    total = width * len(arrays) // 2
    tile = 48 if rows % 48 == 0 else rows
    shape = jax.ShapeDtypeStruct((rows, total), arrays[0].dtype)
    out = pl.BlockSpec((tile, total), lambda i, core: (i, 0))
    return pl.pallas_call(
        functools.partial(split_kernel, sub, places),
        grid_spec=pltpu.PrefetchScalarGridSpec(
            num_scalar_prefetch=1,
            grid=(rows // tile,),
            in_specs=[pl.BlockSpec((tile, width), lambda i, core: (i, 0))] * len(arrays),
            out_specs=[out, out],
        ),
        out_shape=[shape, shape],
    )(my_core().astype(jnp.int32).reshape(1), *arrays)


def join_kernel(sub, places, core_ref, mine, other, *outs):
    def run(core):
        for k, ref in ((core, mine), (1 - core, other)):
            column = 0
            for out in outs:
                for at in places[k]:
                    out[:, at : at + sub] = ref[:, column : column + sub].astype(out.dtype)
                    column += sub

    for core in (0, 1):
        pl.when(core_ref[0] == core)(functools.partial(run, core))


def join_columns(mine, other, count, unit, parts=1):
    rows, total = mine.shape
    width = 2 * total // count
    sub, places = unit_pieces(width, unit, parts)
    tile = 48 if rows % 48 == 0 else rows
    half = pl.BlockSpec((tile, total), lambda i, core: (i, 0))
    return pl.pallas_call(
        functools.partial(join_kernel, sub, places),
        grid_spec=pltpu.PrefetchScalarGridSpec(
            num_scalar_prefetch=1,
            grid=(rows // tile,),
            in_specs=[half, half],
            out_specs=[pl.BlockSpec((tile, width), lambda i, core: (i, 0))] * count,
        ),
        out_shape=[jax.ShapeDtypeStruct((rows, width), F32)] * count,
    )(my_core().astype(jnp.int32).reshape(1), mine, other)


def chip_rows(mine, other):
    got = swap_cores(other)
    return jnp.concatenate([by_core(mine, got), by_core(got, mine)], axis=0)


MESH_ID = pl.DeviceIdType.MESH


def across(place, mask):
    return place + mask - 2 * mask * lax.rem(place // mask, 2)


def highest(at):
    return 1 << (at.bit_length() - 1)


def lowest(at):
    return at & -at


def gather_kernel(chunks, arrays, chips, reps, *refs):
    ins, outs = refs[:arrays], refs[arrays : 2 * arrays]
    along_send, along_recv, rep_send, rep_recv, local_sem = refs[2 * arrays :]
    shard = lax.axis_index("shard")
    chip, core = shard // 2, lax.rem(shard, 2)
    place = lax.axis_index("rep")
    bits = [1 << i for i in range(reps.bit_length() - 1)]
    everyone = range(1, reps)

    def device_at(chip_at):
        return {"shard": 2 * chip_at + core}

    barrier = pltpu.get_barrier_semaphore()
    for by in (1, chips - 1):
        pl.semaphore_signal(
            barrier,
            inc=1,
            device_id=device_at(lax.rem(chip + by, chips)),
            device_id_type=MESH_ID,
        )
    for bit in bits:
        pl.semaphore_signal(
            barrier, inc=1, device_id={"rep": across(place, bit)}, device_id_type=MESH_ID
        )
    pl.semaphore_wait(barrier, 2 + len(bits))

    def block(c, rep_at, chip_at, half=None):
        array, first, columns, sub, split = chunks[c]
        row = (rep_at * chips + chip_at) * sub if split else chip_at * sub
        if half is not None:
            columns = columns // 2
            first = first + half * columns
        return outs[array].at[pl.ds(pl.multiple_of(row, 16), sub), pl.ds(first, columns)]

    def own(c):
        array, first, columns, sub, split = chunks[c]
        row = pl.multiple_of(place * sub, 16) if split else 0
        return ins[array].at[pl.ds(row, sub), pl.ds(first, columns)]

    def along(c, origin, to, direction):
        here = block(c, place, origin)
        return here, pltpu.make_async_remote_copy(
            src_ref=here,
            dst_ref=here,
            send_sem=along_send.at[c, origin, direction],
            recv_sem=along_recv.at[c, origin],
            device_id=device_at(to),
            device_id_type=MESH_ID,
        )

    def first_along(c, to, direction):
        return pltpu.make_async_remote_copy(
            src_ref=own(c),
            dst_ref=block(c, place, chip),
            send_sem=along_send.at[c, chip, direction],
            recv_sem=along_recv.at[c, chip],
            device_id=device_at(to),
            device_id_type=MESH_ID,
        )

    def hop(c, chip_at, at, half):
        bit = at if half is None else (highest(at) if half == 0 else lowest(at))
        here = block(c, across_all(place, at ^ bit), chip_at, half)
        slot = 2 * at + (half or 0)
        return pltpu.make_async_remote_copy(
            src_ref=here,
            dst_ref=here,
            send_sem=rep_send.at[c, chip_at, slot],
            recv_sem=rep_recv.at[c, chip_at, slot],
            device_id={"rep": across(place, bit)},
            device_id_type=MESH_ID,
        )

    def arrival(c, chip_at, at, half):
        here = block(c, across_all(place, at), chip_at, half)
        slot = 2 * at + (half or 0)
        return pltpu.make_async_remote_copy(
            src_ref=here,
            dst_ref=here,
            send_sem=rep_send.at[c, chip_at, slot],
            recv_sem=rep_recv.at[c, chip_at, slot],
            device_id={"rep": place},
            device_id_type=MESH_ID,
        )

    def across_all(at, offset):
        for bit in bits:
            if offset & bit:
                at = across(at, bit)
        return at

    def halves(at):
        return (None,) if at == lowest(at) else (0, 1)

    def local_copies(c):
        array, first, columns, sub, split = chunks[c]
        copies = []
        for part in range(reps if split else 1):
            copies.append(
                pltpu.make_async_copy(
                    ins[array].at[pl.ds(part * sub, sub), pl.ds(first, columns)],
                    block(c, part, chip),
                    local_sem.at[c, part],
                )
            )
        return copies

    def others(run):
        def one(by, carry):
            run(lax.rem(chip + by, chips))
            return carry

        lax.fori_loop(1, chips, one, 0)

    def begin(c):
        @pl.when(chip < chips - 1)
        def _():
            first_along(c, chip + 1, 0).start()

        @pl.when(chip > 0)
        def _():
            first_along(c, chip - 1, 1).start()

        for copy in local_copies(c):
            copy.start()

    def spread(c, origin):
        if chunks[c][4]:
            for bit in bits:
                hop(c, origin, bit, None).start()

    def arrived(c, by):
        @pl.when(chip - by >= 0)
        def _():
            along(c, chip - by, chip, 0)[1].wait_recv()

            @pl.when(chip < chips - 1)
            def _():
                along(c, chip - by, chip + 1, 0)[1].start()

            spread(c, chip - by)

        @pl.when(chip + by < chips)
        def _():
            along(c, chip + by, chip, 1)[1].wait_recv()

            @pl.when(chip > 0)
            def _():
                along(c, chip + by, chip - 1, 1)[1].start()

            spread(c, chip + by)

    def passed(c, level):
        if not chunks[c][4]:
            return

        def run(origin):
            for at in everyone:
                if at.bit_count() == level:
                    for half in halves(at):
                        arrival(c, origin, at, half).wait_recv()
            for at in everyone:
                if at.bit_count() == level + 1:
                    for half in halves(at):
                        hop(c, origin, at, half).start()

        others(run)

    def end(c):
        @pl.when(chip < chips - 1)
        def _():
            first_along(c, chip + 1, 0).wait_send()

        @pl.when(chip > 0)
        def _():
            first_along(c, chip - 1, 1).wait_send()

        for copy in local_copies(c):
            copy.wait()
        for by in range(1, chips):

            @pl.when((chip - by >= 0) & (chip < chips - 1))
            def _(by=by):
                along(c, chip - by, chip + 1, 0)[1].wait_send()

            @pl.when((chip + by < chips) & (chip > 0))
            def _(by=by):
                along(c, chip + by, chip - 1, 1)[1].wait_send()

        if chunks[c][4]:

            def run(origin):
                for at in everyone:
                    for half in halves(at):
                        hop(c, origin, at, half).wait_send()

            others(run)

    stages = (
        [begin]
        + [functools.partial(arrived, by=by) for by in range(1, chips)]
        + [functools.partial(passed, level=level) for level in range(1, len(bits) + 1)]
        + [end]
    )
    for tick in range(len(chunks) + (len(stages) - 1) * LAG):
        for at, stage in enumerate(stages):
            if 0 <= tick - at * LAG < len(chunks):
                stage(tick - at * LAG)


def chip_groups():
    count = lax.axis_size("shard")
    return [list(range(core, count, 2)) for core in (0, 1)]


def gather_plain(array, split):
    if split:
        part = array.shape[0] // lax.axis_size("rep")
        array = lax.dynamic_slice_in_dim(array, lax.axis_index("rep") * part, part, 0)
    array = lax.all_gather(array, "shard", axis=0, tiled=True, axis_index_groups=chip_groups())
    return lax.all_gather(array, "rep", axis=0, tiled=True) if split else array


def reduce_plain(whole):
    part = lax.psum_scatter(whole, "rep", scatter_dimension=0, tiled=True)
    part = lax.psum_scatter(
        part, "shard", scatter_dimension=0, tiled=True, axis_index_groups=chip_groups()
    )
    return lax.all_gather(part, "rep", axis=0, tiled=True)


def gather_all(arrays, splits, widths):
    reps, chips = lax.axis_size("rep"), lax.axis_size("shard") // 2
    if any(split and array.shape[0] // reps % 16 for array, split in zip(arrays, splits)):
        return [gather_plain(array, split) for array, split in zip(arrays, splits)]
    chunks = []
    for i, (array, split, wide) in enumerate(zip(arrays, splits, widths)):
        sub = array.shape[0] // reps if split else array.shape[0]
        for first in range(0, array.shape[1], wide):
            chunks.append((i, first, min(wide, array.shape[1] - first), sub, split))
    slots = 2 * reps
    count = len(chunks)
    return pl.pallas_call(
        functools.partial(gather_kernel, chunks, len(arrays), chips, reps),
        in_specs=[pl.BlockSpec(memory_space=pltpu.VMEM)] * len(arrays),
        out_specs=[pl.BlockSpec(memory_space=pl.ANY)] * len(arrays),
        out_shape=[
            jax.ShapeDtypeStruct((a.shape[0] * chips, a.shape[1]), a.dtype) for a in arrays
        ],
        scratch_shapes=[
            pltpu.SemaphoreType.DMA((count, chips, 2)),
            pltpu.SemaphoreType.DMA((count, chips)),
            pltpu.SemaphoreType.DMA((count, chips, slots)),
            pltpu.SemaphoreType.DMA((count, chips, slots)),
            pltpu.SemaphoreType.DMA((count, reps)),
        ],
        compiler_params=pltpu.CompilerParams(
            collective_id=0, has_side_effects=True, vmem_limit_bytes=40 * 1024 * 1024
        ),
        cost_estimate=pl.CostEstimate(
            flops=0, bytes_accessed=sum(70 * a.size for a in arrays), transcendentals=0
        ),
    )(*arrays)


def reduce_kernel(chunks, counts, chips, *refs):
    n_left, n_right, n_given, n_out = counts
    n = len(chunks)
    refs = list(refs)

    def take(count):
        taken = refs[:count]
        del refs[:count]
        return taken

    lefts, rights, givens = take(n_left), take(n_right), take(n_given)
    outs, first_in, second_in, chip_in = take(n_out), take(n), take(n), take(n)
    right_buf, big_left, first_out, first_loc, second_out, second_loc = take(6)
    chip_out, chip_loc, own_out = take(3)
    send, recv, chip_send, chip_recv, hop_send, hop_recv, local = take(7)
    shard = lax.axis_index("shard")
    chip, core = shard // 2, lax.rem(shard, 2)
    place = lax.axis_index("rep")
    bits = (1, 2)

    def device_at(chip_at):
        return {"shard": 2 * chip_at + core}

    barrier = pltpu.get_barrier_semaphore()
    for by in range(1, chips):
        pl.semaphore_signal(
            barrier,
            inc=1,
            device_id=device_at(lax.rem(chip + by, chips)),
            device_id_type=MESH_ID,
        )
    for bit in bits:
        pl.semaphore_signal(
            barrier, inc=1, device_id={"rep": across(place, bit)}, device_id_type=MESH_ID
        )
    pl.semaphore_wait(barrier, chips - 1 + len(bits))

    def rep_at(offset):
        at = place
        for bit in bits:
            if offset & bit:
                at = across(at, bit)
        return at

    def masks(c):
        return bits[::-1] if chunks[c]["flip"] else bits

    def rows_of(c):
        return chips * chunks[c]["sub"]

    def right_copy(c):
        k = chunks[c]
        return pltpu.make_async_copy(
            rights[k["right"]].at[:, pl.ds(k["first"], k["wide"])],
            right_buf.at[c % 6, :, pl.ds(0, k["wide"])],
            local.at[c, 0],
        )

    def left_copy(c):
        return pltpu.make_async_copy(lefts[chunks[c]["left"]], big_left, local.at[c, 1])

    def exchange(c, turn):
        k, rows = chunks[c], rows_of(c)
        source, target = ((first_out, first_in), (second_out, second_in))[turn]
        return pltpu.make_async_remote_copy(
            src_ref=source.at[c % 3, :, pl.ds(0, rows), pl.ds(0, k["wide"])],
            dst_ref=target[c],
            send_sem=send.at[c, turn],
            recv_sem=recv.at[c, turn],
            device_id={"rep": across(place, masks(c)[turn])},
            device_id_type=MESH_ID,
        )

    def arrived_copy(c, turn):
        k, rows = chunks[c], rows_of(c)
        source = (first_in, second_in)[turn][c]
        target = (first_loc.at[c % 4], second_loc.at[c % 2])[turn]
        return pltpu.make_async_copy(
            source, target.at[:, pl.ds(0, rows), pl.ds(0, k["wide"])], local.at[c, 2 + turn]
        )

    def tiles(c, run):
        wide = chunks[c]["wide"]
        tile = 256 if wide % 256 == 0 else 128

        def one(i, carry):
            run(pl.ds(pl.multiple_of(i * tile, tile), tile))
            return carry

        lax.fori_loop(0, wide // tile, one, 0)

    def product(c, offset, target, arrivals):
        k, rows = chunks[c], rows_of(c)
        at = rep_at(offset)

        def run(columns):
            if k["given"] is not None:
                total = givens[k["given"]][at, :, columns].astype(F32)
            else:
                right = right_buf[c % 6, :, columns]
                if k["big"]:
                    total = jnp.dot(big_left[at], right, preferred_element_type=F32)
                else:
                    left = lefts[k["left"]][:, pl.ds(pl.multiple_of(at * rows, 128), rows)]
                    total = matmul_left(left, right)
            for ref, index in arrivals:
                total = total + ref[index + (pl.ds(0, rows), columns)].astype(F32)
            target[0][target[1] + (pl.ds(0, rows), columns)] = total.astype(BF16)

        tiles(c, run)

    def load(c):
        if chunks[c]["given"] is None:
            right_copy(c).start()
            if chunks[c]["load"]:
                left_copy(c).start()

    def send_first(c):
        if chunks[c]["given"] is None:
            right_copy(c).wait()
            if chunks[c]["load"]:
                left_copy(c).wait()
        one, two = masks(c)
        product(c, one, (first_out, (c % 3, 0)), [])
        product(c, one ^ two, (first_out, (c % 3, 1)), [])
        exchange(c, 0).start()

    def take_first(c):
        exchange(c, 0).wait_recv()
        arrived_copy(c, 0).start()

    def send_second(c):
        arrived_copy(c, 0).wait()
        product(c, masks(c)[1], (second_out, (c % 3, 0)), [(first_loc, (c % 4, 1))])
        exchange(c, 1).start()
        exchange(c, 0).wait_send()

    def take_second(c):
        exchange(c, 1).wait_recv()
        arrived_copy(c, 1).start()

    def to_chip(c, by):
        k = chunks[c]
        at = lax.rem(chip + by, chips)
        row = pl.multiple_of(at * k["sub"], 16)
        return pltpu.make_async_remote_copy(
            src_ref=chip_out.at[c % 3, pl.ds(row, k["sub"]), pl.ds(0, k["wide"])],
            dst_ref=chip_in[c].at[by - 1],
            send_sem=chip_send.at[c, by - 1],
            recv_sem=chip_recv.at[c, by - 1],
            device_id=device_at(at),
            device_id_type=MESH_ID,
        )

    def send_chips(c):
        arrived_copy(c, 1).wait()
        product(
            c, 0, (chip_out, (c % 3,)), [(first_loc, (c % 4, 0)), (second_loc, (c % 2, 0))]
        )
        for by in range(1, chips):
            to_chip(c, by).start()
        exchange(c, 1).wait_send()

    def chips_copy(c):
        k = chunks[c]
        return pltpu.make_async_copy(
            chip_in[c],
            chip_loc.at[c % 2, :, pl.ds(0, k["sub"]), pl.ds(0, k["wide"])],
            local.at[c, 4],
        )

    def take_chips(c):
        for by in range(1, chips):
            to_chip(c, by).wait_recv()
        chips_copy(c).start()

    def out_rows(c, offset, half=None):
        k = chunks[c]
        first, wide = k["place"], k["wide"]
        if half is not None:
            wide = wide // 2
            first = first + half * wide
        row = pl.multiple_of(rep_at(offset) * k["sub"], 16)
        return outs[k["out"]].at[pl.ds(row, k["sub"]), pl.ds(first, wide)]

    def own_rows_of(c):
        k = chunks[c]
        return own_out.at[c % 3, pl.ds(0, k["sub"]), pl.ds(0, k["wide"])]

    def own_copy(c):
        return pltpu.make_async_copy(own_rows_of(c), out_rows(c, 0), local.at[c, 5])

    def hop(c, at, half):
        bit = at if at in bits else (2 if half != 1 else 1)
        here = out_rows(c, at ^ bit, half)
        slot = 2 * at + (half or 0)
        return pltpu.make_async_remote_copy(
            src_ref=own_rows_of(c) if at in bits else here,
            dst_ref=here,
            send_sem=hop_send.at[c, slot],
            recv_sem=hop_recv.at[c, slot],
            device_id={"rep": across(place, bit)},
            device_id_type=MESH_ID,
        )

    def arrival(c, at, half):
        here = out_rows(c, at, half)
        slot = 2 * at + (half or 0)
        return pltpu.make_async_remote_copy(
            src_ref=here,
            dst_ref=here,
            send_sem=hop_send.at[c, slot],
            recv_sem=hop_recv.at[c, slot],
            device_id={"rep": across(place, 1)},
            device_id_type=MESH_ID,
        )

    def far_halves(c):
        return (0, 1) if chunks[c]["wide"] % 256 == 0 else (None,)

    def send_sums(c):
        k = chunks[c]
        chips_copy(c).wait()
        row = pl.multiple_of(chip * k["sub"], 16)

        def run(columns):
            total = chip_out[c % 3, pl.ds(row, k["sub"]), columns].astype(F32)
            for by in range(1, chips):
                total = total + chip_loc[c % 2, by - 1, pl.ds(0, k["sub"]), columns].astype(F32)
            own_out[c % 3, pl.ds(0, k["sub"]), columns] = total.astype(BF16)

        tiles(c, run)
        for bit in bits:
            hop(c, bit, None).start()
        own_copy(c).start()
        for by in range(1, chips):
            to_chip(c, by).wait_send()

    def pass_sums(c):
        for bit in bits:
            arrival(c, bit, None).wait_recv()
        for half in far_halves(c):
            hop(c, 3, half).start()

    def end(c):
        own_copy(c).wait()
        for bit in bits:
            hop(c, bit, None).wait_send()
        for half in far_halves(c):
            arrival(c, 3, half).wait_recv()
            hop(c, 3, half).wait_send()

    stages = [
        load,
        send_first,
        take_first,
        send_second,
        take_second,
        send_chips,
        take_chips,
        send_sums,
        pass_sums,
        end,
    ]
    for tick in range(n + len(stages) - 1):
        for at, stage in enumerate(stages):
            if 0 <= tick - at < n:
                stage(tick - at)


def reduce_all(products):
    reps, chips = lax.axis_size("rep"), lax.axis_size("shard") // 2
    depth = max(left.shape[0] for left, _, _ in products if left is not None)
    if reps != 4 or any(
        (given[0].shape[1] if left is None else left.shape[1] // reps) // chips % 16
        for left, given, _ in products
    ):
        results = []
        for left, given, _ in products:
            if left is None:
                whole = given[0].reshape(-1, given[0].shape[2])
            else:
                whole = jnp.concatenate(
                    [matmul_left(left, right).astype(BF16) for right in given], axis=1
                )
            results.append(reduce_plain(whole))
        return results
    lefts, rights, givens, chunks, outs = [], [], [], [], []
    subs = [
        (given[0].shape[1] if left is None else left.shape[1] // reps) // chips
        for left, given, _ in products
    ]
    largest = max(subs)
    for (left, parts, wide), sub in zip(products, subs):
        total = sum(part.shape[-1] for part in parts)
        outs.append(jax.ShapeDtypeStruct((reps * sub, total), BF16))
        first_right = len(rights)
        if left is not None:
            lefts.append(left.T.reshape(reps, chips * sub, depth) if sub == largest else left)
            rights.extend(parts)
        else:
            givens.extend(parts)
        before = 0
        mine = []
        for i, part in enumerate(parts):
            row = []
            for first in range(0, part.shape[-1], wide):
                row.append(
                    dict(
                        left=len(lefts) - 1,
                        given=len(givens) - 1 if left is None else None,
                        right=first_right + i,
                        first=first,
                        wide=min(wide, part.shape[-1] - first),
                        sub=sub,
                        out=len(outs) - 1,
                        place=before + first,
                        big=sub == largest,
                        load=False,
                    )
                )
            mine.append(row)
            before += part.shape[-1]
        mine = [chunk for group in zip(*mine) for chunk in group]
        mine[0]["load"] = sub == largest
        chunks += mine
    for i, chunk in enumerate(chunks):
        chunk["flip"] = i % 2
    n = len(chunks)
    rows = max(subs) * chips
    wide = max(chunk["wide"] for chunk in chunks)
    hbm = pl.BlockSpec(memory_space=pl.ANY)
    vmem = pl.BlockSpec(memory_space=pltpu.VMEM)
    big = {chunk["left"] for chunk in chunks if chunk["big"]}

    def landing(blocks, sub_only=False):
        return [
            jax.ShapeDtypeStruct(
                (blocks, c["sub"] if sub_only else chips * c["sub"], c["wide"]), BF16
            )
            for c in chunks
        ]

    shapes = outs + landing(2) + landing(1) + landing(chips - 1, True)
    results = pl.pallas_call(
        functools.partial(
            reduce_kernel, chunks, (len(lefts), len(rights), len(givens), len(outs)), chips
        ),
        in_specs=[hbm if i in big else vmem for i in range(len(lefts))]
        + [hbm] * len(rights)
        + [vmem] * len(givens),
        out_specs=[hbm] * len(shapes),
        out_shape=shapes,
        scratch_shapes=[
            pltpu.VMEM((6, depth, wide), BF16),
            pltpu.VMEM((reps, rows, depth), BF16),
            pltpu.VMEM((3, 2, rows, wide), BF16),
            pltpu.VMEM((4, 2, rows, wide), BF16),
            pltpu.VMEM((3, 1, rows, wide), BF16),
            pltpu.VMEM((2, 1, rows, wide), BF16),
            pltpu.VMEM((3, rows, wide), BF16),
            pltpu.VMEM((2, chips - 1, max(subs), wide), BF16),
            pltpu.VMEM((3, max(subs), wide), BF16),
            pltpu.SemaphoreType.DMA((n, 2)),
            pltpu.SemaphoreType.DMA((n, 2)),
            pltpu.SemaphoreType.DMA((n, chips - 1)),
            pltpu.SemaphoreType.DMA((n, chips - 1)),
            pltpu.SemaphoreType.DMA((n, 8)),
            pltpu.SemaphoreType.DMA((n, 8)),
            pltpu.SemaphoreType.DMA((n, 6)),
        ],
        compiler_params=pltpu.CompilerParams(
            collective_id=1, has_side_effects=True, vmem_limit_bytes=62 * 1024 * 1024
        ),
        cost_estimate=pl.CostEstimate(
            flops=0,
            bytes_accessed=sum(128 * shape.size for shape in outs),
            transcendentals=0,
        ),
    )(*lefts, *rights, *givens)
    return results[: len(outs)]


def own_rows(rows):
    part = rows.shape[0] // 2
    core = my_core()
    mine = lax.dynamic_slice_in_dim(rows, core * part, part, 0)
    return mine, swap_cores(lax.dynamic_slice_in_dim(rows, (1 - core) * part, part, 0))


ROOT = math.sqrt(2.0 / math.pi)


def gelu_parts(v):
    inner = jnp.tanh(ROOT * (v + 0.044715 * v * v * v))
    value = 0.5 * v * (1.0 + inner)
    slope = 0.5 * (1.0 + inner) + 0.5 * v * (1.0 - inner * inner) * ROOT * (
        1.0 + 3.0 * 0.044715 * v * v
    )
    return value, slope


def one_minus_exp(v):
    series = 1.0 + v / 8.0
    for order in (7.0, 6.0, 5.0, 4.0, 3.0, 2.0):
        series = 1.0 + v * series * (1.0 / order)
    return -v * series


def sigmoid(v):
    return 1.0 / (1.0 + jnp.exp(-v))


def scan_rows(a, b, a_ref, b_ref, cum_ref, out_ref, reverse):
    rows, lanes = a.shape
    place = lax.rem(lax.broadcasted_iota(jnp.int32, (rows, lanes), 0), 8)
    for k in (1, 2, 4):
        by = rows - k if reverse else k
        inside = place < 8 - k if reverse else place >= k
        a_before = jnp.where(inside, pltpu.roll(a, by, 0), 1.0)
        b_before = jnp.where(inside, pltpu.roll(b, by, 0), 0.0)
        b = a * b_before + b
        a = a * a_before
    a_ref[...] = a
    b_ref[...] = b
    groups = rows // 8
    last = 0 if reverse else 7

    def step(turn, carry):
        carry_cum, carry_out = carry
        group = groups - 1 - turn if reverse else turn
        where = pl.ds(pl.multiple_of(group * 8, 8), 8)
        out = b_ref[where, :] + a_ref[where, :] * carry_out
        cum = a_ref[where, :] * carry_cum
        out_ref[0, where, :] = out
        cum_ref[0, where, :] = cum
        return (
            jnp.broadcast_to(cum[last : last + 1], (8, lanes)),
            jnp.broadcast_to(out[last : last + 1], (8, lanes)),
        )

    lax.fori_loop(
        0, groups, step, (jnp.ones((8, lanes), F32), jnp.zeros((8, lanes), F32)), unroll=4
    )


def shifted_rows(x, tail, by):
    return pltpu.roll(jnp.concatenate([tail, x], axis=0), by, 0)[8:] if by else x


def conv_rows(branch, tail, taps):
    return sum(taps[j : j + 1] * shifted_rows(branch, tail, j) for j in range(taps.shape[0]))


def by_blocks(low, weights, block, contract=0):
    parts = []
    for i in range(low.shape[1] // block):
        parts.append(
            lax.dot_general(
                low[:, i * block : (i + 1) * block],
                weights[i * block : (i + 1) * block],
                (((1,), (contract,)), ((), ())),
                preferred_element_type=F32,
            )
        )
    return jnp.concatenate(parts, axis=1)


def lru_forward_kernel(
    block, branch_ref, tail_ref, rate_ref, input_ref, taps_ref, decay_ref,
    coef_ref, cum_ref, state_ref, a_ref, b_ref,
):
    conv = conv_rows(branch_ref[0], tail_ref[0], taps_ref[...])
    low = conv.astype(BF16)
    log_coef = -8.0 * sigmoid(by_blocks(low, rate_ref[...], block)) * decay_ref[...]
    coef = jnp.exp(log_coef)
    gate = sigmoid(by_blocks(low, input_ref[...], block))
    drive = jnp.sqrt(one_minus_exp(2.0 * log_coef)) * gate * conv
    coef_ref[0] = coef
    scan_rows(coef, drive, a_ref, b_ref, cum_ref, state_ref, False)


def lru_adjoint_kernel(
    gated_ref, coef_ref, cum_ref, local_ref, start_ref, back_ref,
    later_ref, adjoint_ref, gated_back_ref, a_ref, b_ref,
):
    value, slope = gelu_parts(gated_ref[0])
    back = back_ref[0].astype(F32)
    state = local_ref[0] + cum_ref[0] * start_ref[0][:1]
    gated_back_ref[0] = (back * state * slope).astype(BF16)
    coef = coef_ref[0]
    rows = coef.shape[0]
    last = lax.broadcasted_iota(jnp.int32, coef.shape, 0) == rows - 1
    coef_next = jnp.where(last, 1.0, pltpu.roll(coef, rows - 1, 0))
    scan_rows(coef_next, back * value, a_ref, b_ref, later_ref, adjoint_ref, True)


def lru_backward_kernel(
    block, branch_ref, tail_ref, rate_ref, input_ref, taps_ref, decay_ref,
    cum_ref, local_ref, start_ref, later_ref, adjoint_ref, carry_ref,
    branch_back_ref, first_ref, last_ref, rate_grad_ref, input_grad_ref, taps_grad_ref, decay_grad_ref,
):
    branch, tail, taps, decay = branch_ref[0], tail_ref[0], taps_ref[...], decay_ref[...]
    rows = branch.shape[0]
    conv = conv_rows(branch, tail, taps)
    low = conv.astype(BF16)
    rate = sigmoid(by_blocks(low, rate_ref[...], block))
    gate = sigmoid(by_blocks(low, input_ref[...], block))
    log_coef = -8.0 * rate * decay
    coef = jnp.exp(log_coef)
    root = jnp.sqrt(one_minus_exp(2.0 * log_coef))
    start = start_ref[0][:1]
    state = local_ref[0] + cum_ref[0] * start
    first = lax.broadcasted_iota(jnp.int32, state.shape, 0) == 0
    before = jnp.where(first, start, pltpu.roll(state, 1, 0))
    adjoint = adjoint_ref[0] + later_ref[0] * carry_ref[0][:1]
    back_root = adjoint * gate * conv
    back_log = (adjoint * before - back_root * coef / root) * coef
    back_rate = back_log * (-8.0 * decay) * rate * (1.0 - rate)
    back_gate = adjoint * root * conv * gate * (1.0 - gate)
    rate_low, gate_low = back_rate.astype(BF16), back_gate.astype(BF16)
    back_conv = (
        adjoint * root * gate
        + by_blocks(rate_low, rate_ref[...], block, 1)
        + by_blocks(gate_low, input_ref[...], block, 1)
    )

    def block_grads(back):
        return jnp.concatenate(
            [
                lax.dot_general(
                    low[:, i : i + block],
                    back[:, i : i + block],
                    (((0,), (0,)), ((), ())),
                    preferred_element_type=F32,
                )
                for i in range(0, low.shape[1], block)
            ],
            axis=0,
        )

    taps_grad = jnp.concatenate(
        [
            jnp.sum(back_conv * shifted_rows(branch, tail, j), axis=0, keepdims=True)
            for j in range(taps.shape[0])
        ],
        axis=0,
    )
    grads = (
        (rate_grad_ref, block_grads(rate_low)),
        (input_grad_ref, block_grads(gate_low)),
        (taps_grad_ref, taps_grad),
        (decay_grad_ref, jnp.sum(back_log * (-8.0 * rate), axis=0, keepdims=True)),
    )

    @pl.when(pl.program_id(1) == 0)
    def _():
        for ref, grad in grads:
            ref[...] = grad

    @pl.when(pl.program_id(1) > 0)
    def _():
        for ref, grad in grads:
            ref[...] += grad

    extended = jnp.concatenate([back_conv, jnp.zeros((8, branch.shape[1]), F32)], axis=0)
    branch_back = sum(
        taps[j : j + 1] * (pltpu.roll(extended, rows + 8 - j, 0)[:rows] if j else back_conv)
        for j in range(taps.shape[0])
    )
    branch_back_ref[0] = branch_back.astype(BF16)
    first_ref[0] = back_conv[:8]
    last_ref[0] = branch_back[rows - 8 :]


def lru_call(kernel, arrays, outs, rows, scratch=()):
    lanes = 256
    kinds = {
        "first": ((1, rows, lanes), lambda i, b: (b, 0, i)),
        "second": ((1, rows, lanes), None),
        "edge": ((1, 8, lanes), lambda i, b: (b, 0, i)),
        "weight": ((lanes, 128), lambda i, b: (i, 0)),
        "taps": ((4, lanes), lambda i, b: (0, i)),
        "row": ((1, lanes), lambda i, b: (0, i)),
    }
    width = max(a.shape[-1] for a, kind in outs if kind == "first")

    def spec(kind):
        shape, place = kinds[kind]
        if kind == "second":
            place = lambda i, b: (b, 0, i + width // lanes)
        return pl.BlockSpec(shape, place)

    return pl.pallas_call(
        kernel,
        grid=(width // lanes, 2),
        in_specs=[spec(kind) for _, kind in arrays],
        out_specs=[spec(kind) for _, kind in outs],
        out_shape=[a for a, _ in outs],
        scratch_shapes=list(scratch),
        compiler_params=pltpu.CompilerParams(vmem_limit_bytes=56 * 1024 * 1024),
        cost_estimate=pl.CostEstimate(
            flops=0, bytes_accessed=16 * rows * width * 4, transcendentals=0
        ),
    )(*[a for a, _ in arrays])


def carried_in(prod, part, reverse):
    size = lax.axis_size("rep")
    pair = jnp.stack([prod, part])
    total = jnp.zeros_like(part)
    through = jnp.ones_like(prod)
    place = lax.axis_index("rep")
    ahead = size - 1 - place if reverse else place
    for distance in range(1, size):
        got = shift_rep(pair, -distance if reverse else distance)
        total = total + through * got[1]
        through = jnp.where(ahead >= distance, through * got[0], through)
    return total


def block_probs(query, keys, lowest):
    scores = lax.dot_general(
        query, keys, (((1,), (1,)), ((), ())), preferred_element_type=F32
    ) * (1.0 / math.sqrt(query.shape[1]))
    row = lax.broadcasted_iota(jnp.int32, scores.shape, 0)
    column = lax.broadcasted_iota(jnp.int32, scores.shape, 1)
    allowed = (column > row) & (column <= row + WINDOW) & (column >= lowest)
    scores = jnp.where(allowed, scores, -1e30)
    powers = jnp.exp(scores - jnp.max(scores, axis=1, keepdims=True))
    return powers * (1.0 / jnp.sum(powers, axis=1, keepdims=True))


def attention_kernel(start_ref, query_ref, kv_ref, out_ref):
    rows, size = query_ref.shape
    block = min(256, rows)
    for first in range(0, rows, block):
        keys = kv_ref[first : first + block + WINDOW, :size]
        values = kv_ref[first : first + block + WINDOW, size:]
        probs = block_probs(
            query_ref[first : first + block, :], keys, WINDOW - first - start_ref[0]
        )
        out_ref[first : first + block, :] = jnp.dot(
            probs.astype(BF16), values, preferred_element_type=F32
        ).astype(BF16)


def attention_back_kernel(start_ref, query_ref, back_ref, kv_ref, query_back_ref, kv_back_ref):
    rows, size = query_ref.shape
    block = min(256, rows)
    scale = 1.0 / math.sqrt(size)

    @pl.when(pl.program_id(0) == 0)
    def _():
        kv_back_ref[...] = jnp.zeros_like(kv_back_ref)

    for first in range(0, rows, block):
        here = slice(first, first + block + WINDOW)
        keys, values = kv_ref[here, :size], kv_ref[here, size:]
        query = query_ref[first : first + block, :]
        back = back_ref[first : first + block, :]
        probs = block_probs(query, keys, WINDOW - first - start_ref[0])
        back_probs = lax.dot_general(
            back, values, (((1,), (1,)), ((), ())), preferred_element_type=F32
        )
        prob_dot = jnp.sum(probs * back_probs, axis=1, keepdims=True)
        back_scores = (probs * (back_probs - prob_dot)).astype(BF16)
        query_back_ref[first : first + block, :] = (
            jnp.dot(back_scores, keys, preferred_element_type=F32) * scale
        ).astype(BF16)
        kv_back_ref[here, :size] += (
            lax.dot_general(
                back_scores, query, (((0,), (0,)), ((), ())), preferred_element_type=F32
            )
            * scale
        )
        kv_back_ref[here, size:] += lax.dot_general(
            probs.astype(BF16), back, (((0,), (0,)), ((), ())), preferred_element_type=F32
        )


def attention_call(kernel, start, by_head, kv, outs):
    rows, width = by_head[0].shape
    size = kv.shape[1] // 2
    head = pl.BlockSpec((rows, size), lambda h, start: (0, h))
    whole = pl.BlockSpec(kv.shape, lambda h, start: (0, 0))
    return pl.pallas_call(
        kernel,
        grid_spec=pltpu.PrefetchScalarGridSpec(
            num_scalar_prefetch=1,
            grid=(width // size,),
            in_specs=[head] * len(by_head) + [whole],
            out_specs=[head, whole][: len(outs)],
        ),
        out_shape=outs,
        compiler_params=pltpu.CompilerParams(vmem_limit_bytes=56 * 1024 * 1024),
        cost_estimate=pl.CostEstimate(
            flops=12 * rows * width * WINDOW,
            bytes_accessed=64 * 1024 * 1024,
            transcendentals=0,
        ),
    )(jnp.reshape(start, (1,)), *by_head, kv)


def with_sibling(x):
    return jnp.concatenate([x, swap_cores(x)], axis=0)


def sum_parts(parts):
    rows = parts.shape[0] // 2
    return parts[:rows] + swap_cores(parts[rows:])


def mlp_forward(resid, norm_gain, in_w, down_w):
    normed = with_sibling(rms_norm(resid, norm_gain).astype(BF16))
    middle = in_w.shape[1] // 2
    both = matmul(normed, in_w)
    gate_pre, up_pre = both[:, :middle], both[:, middle:]
    hidden = mlp_middle(gate_pre, up_pre).astype(BF16)
    return resid + sum_parts(matmul(hidden, down_w)), (normed, gate_pre, up_pre, hidden)


def mlp_backward(resid, norm_gain, in_w, down_w, kept_vals, back_out):
    normed, gate_pre, up_pre, hidden = kept_vals
    out_low = with_sibling(back_out.astype(BF16))
    back_hidden = rounded(matmul_right(out_low, down_w))
    back_gate, back_up = jax.vjp(mlp_middle, gate_pre, up_pre)[1](back_hidden)
    gate_low = back_gate.astype(BF16)
    up_low = back_up.astype(BF16)
    back_normed = sum_parts(matmul_right(jnp.concatenate([gate_low, up_low], axis=1), in_w))
    back_resid, grad_gain = jax.vjp(rms_norm, resid, norm_gain)[1](back_normed)
    return (back_out + back_resid, (grad_gain, (normed, gate_low), (normed, up_low), (hidden, out_low)))


def on_device(
    tokens_in,
    lengths,
    cotangent,
    attn_norm,
    query_proj,
    key_proj,
    value_proj,
    attn_out,
    first_norm,
    first_gate,
    first_up,
    first_down,
    mixer_norm,
    branch_proj,
    gated_proj,
    conv_taps,
    rate_gate,
    input_gate,
    decay_rate,
    mixer_out,
    second_norm,
    second_gate,
    second_up,
    second_down,
):
    row_count = tokens_in.shape[1]
    width = tokens_in.shape[2]
    shards = lax.axis_size("shard")
    reps = lax.axis_size("rep")
    chips = shards // 2
    core = my_core()
    start_row = lax.axis_index("rep") * row_count
    positions = start_row + jnp.arange(row_count, dtype=jnp.int32)
    valid_mask = (positions < lengths[0]).astype(F32)[:, None]

    piece = width // chips // reps
    spot = lax.broadcasted_iota(jnp.int32, (width, width), 1)
    natural = (
        lax.rem(spot // piece, chips) * (piece * reps)
        + (spot // (piece * chips)) * piece
        + lax.rem(spot, piece)
    )
    to_order = (lax.broadcasted_iota(jnp.int32, (width, width), 0) == natural).astype(BF16)

    def ordered(x):
        return matmul(x, to_order)

    def unordered(x):
        return matmul_right(x, to_order)

    head_size = key_proj.shape[1]
    half = query_proj.shape[1] // 2
    gain_columns = jnp.stack([attn_norm, first_norm, mixer_norm, second_norm], axis=1)
    gain_columns = jnp.pad(gain_columns, ((0, 0), (0, 128 - 4)))
    qkv_halves = (
        jnp.concatenate([query_proj[:, :half], key_proj, gain_columns], axis=1),
        jnp.concatenate([query_proj[:, half:], value_proj, gain_columns], axis=1),
    )
    out_ordered = ordered(attn_out).astype(BF16)
    out_halves = out_ordered[:, : width // 2], out_ordered[:, width // 2 :]
    attn_halves = tuple(jnp.concatenate(both, axis=1) for both in zip(qkv_halves, out_halves))
    qkv_width = half + head_size
    ff_unit = first_down.shape[0]
    lru_unit = mixer_out.shape[0]

    block_width = rate_gate.shape[1]
    tap_count = conv_taps.shape[1]
    spare = block_width - tap_count - 1
    second_chip = chip_rows(*split_columns((second_gate, second_up), ff_unit, reps))
    attn_halves, second_chip = lax.optimization_barrier((attn_halves, second_chip))
    second_in_w = gather_plain(second_chip, True)
    attn_wide, first_in_w, first_down_w, lru_in_w, mix_wide, second_down_w = gather_all(
        (
            chip_rows(by_core(*attn_halves), by_core(*attn_halves[::-1])),
            chip_rows(*split_columns((first_gate, first_up), ff_unit, reps)),
            ordered(first_down).astype(BF16),
            chip_rows(*split_columns((branch_proj, gated_proj), lru_unit)),
            jnp.concatenate(
                [
                    rate_gate,
                    input_gate,
                    conv_taps,
                    decay_rate[:, None],
                    jnp.zeros((lru_unit, spare), BF16),
                    ordered(mixer_out).astype(BF16),
                ],
                axis=1,
            ),
            ordered(second_down).astype(BF16),
        ),
        (True, True, True, True, False, True),
        (1792, 1536, 1536, 1024, 1920, 1536),
    )
    qkv_own = attn_wide[:, :qkv_width]
    gains = attn_wide[:, qkv_width : qkv_width + 128].astype(F32)
    gain_attn, gain_first, gain_mix, gain_second = (gains[:, i] for i in range(4))
    attn_own = attn_wide[:, qkv_width + 128 :]
    qkv_sib = swap_cores(qkv_own)
    attn_sib = swap_cores(attn_own)

    small_w = mix_wide[:, : 3 * block_width]
    mix_w = mix_wide[:, 3 * block_width :]

    inputs = ordered(tokens_in.reshape(row_count, width))
    attn_normed = rms_norm(inputs, gain_attn).astype(BF16)
    qkv_mine = matmul(attn_normed, qkv_own).astype(BF16)
    qkv_other = matmul(attn_normed, qkv_sib).astype(BF16)
    qkv_first, qkv_second = by_core(qkv_mine, qkv_other), by_core(qkv_other, qkv_mine)
    query_rows = jnp.concatenate([qkv_first[:, :half], qkv_second[:, :half]], axis=1)
    kv_rows = jnp.concatenate([qkv_first[:, half:], qkv_second[:, half:]], axis=1)
    blocks_behind = -(-WINDOW // row_count)
    behind = blocks_behind * row_count
    kv_win = jnp.concatenate(
        [shift_rep(kv_rows, by) for by in range(blocks_behind, 0, -1) if by < reps]
        + [kv_rows],
        axis=0,
    )
    behind = kv_win.shape[0] - row_count
    (attended,) = attention_call(
        attention_kernel,
        start_row,
        [query_rows],
        kv_win,
        [jax.ShapeDtypeStruct((row_count, width), BF16)],
    )
    attended_low = ordered(attended).astype(BF16)
    out_mine = matmul(attended_low, attn_own)
    out_other = matmul(attended_low, attn_sib)
    resid_one = inputs + jnp.concatenate(
        [by_core(out_mine, out_other), by_core(out_other, out_mine)], axis=1
    )

    middle, first_kept = mlp_forward(resid_one, gain_first, first_in_w, first_down_w)

    conv_w = small_w[:, 2 * block_width : 2 * block_width + tap_count].astype(F32).T
    decay_w = small_w[:, 2 * block_width + tap_count].astype(F32)[None]
    rate_w = small_w[:, :block_width]
    input_w = small_w[:, block_width : 2 * block_width]
    mix_normed = with_sibling(rms_norm(middle, gain_mix).astype(BF16))
    lru_width = lru_in_w.shape[1] // 2
    branch_gated = matmul(mix_normed, lru_in_w).reshape(2, row_count, 2 * lru_width)
    tail_rows = shift_rep(branch_gated[:, row_count - 8 :, :lru_width], 1)
    lru_inputs = [
        (branch_gated, "first"),
        (tail_rows, "edge"),
        (rate_w, "weight"),
        (input_w, "weight"),
        (conv_w, "taps"),
        (decay_w, "row"),
    ]
    wide = (jax.ShapeDtypeStruct((2, row_count, lru_width), F32), "first")
    wide_low = (jax.ShapeDtypeStruct((2, row_count, lru_width), BF16), "first")
    edge = (jax.ShapeDtypeStruct((2, 8, lru_width), F32), "edge")
    scans = [pltpu.VMEM((row_count, 256), F32)] * 2
    lru_coef, cum_coef, local_state = lru_call(
        functools.partial(lru_forward_kernel, block_width),
        lru_inputs,
        [wide, wide, wide],
        row_count,
        scans,
    )
    start_state = carried_in(cum_coef[:, -1], local_state[:, -1], False)
    start_edge = jnp.broadcast_to(start_state[:, None], edge[0].shape)
    gated_act = gelu_tanh(branch_gated[:, :, lru_width:])
    mix_low = ((local_state + cum_coef * start_state[:, None]) * gated_act).astype(BF16)
    mix_low = mix_low.reshape(2 * row_count, lru_width)
    resid_two = middle + sum_parts(matmul(mix_low, mix_w))

    final_rows, second_kept = mlp_forward(
        resid_two, gain_second, second_in_w, second_down_w
    )
    out_tokens = unordered(final_rows.astype(BF16)).astype(BF16).reshape(1, row_count, width)
    back_final = ordered(cotangent.reshape(row_count, width)) * valid_mask
    back_two, second_grads = mlp_backward(
        resid_two,
        gain_second,
        second_in_w,
        second_down_w,
        second_kept,
        back_final,
    )

    down_part = lax.psum_scatter(
        matmul_left(*second_grads[3]).astype(BF16), "rep", scatter_dimension=0, tiled=True
    )
    in_part = lax.psum_scatter(
        matmul_left(
            second_grads[1][0],
            jnp.concatenate([second_grads[1][1], second_grads[2][1]], axis=1),
        ).astype(BF16),
        "rep",
        scatter_dimension=0,
        tiled=True,
    )

    mix_back_low = with_sibling(back_two.astype(BF16))
    back_mixed = matmul_right(mix_back_low, mix_w).astype(BF16).reshape(wide[0].shape)
    later_prod, local_adjoint, gated_back_low = lru_call(
        lru_adjoint_kernel,
        [
            (branch_gated, "second"),
            (lru_coef, "first"),
            (cum_coef, "first"),
            (local_state, "first"),
            (start_edge, "edge"),
            (back_mixed, "first"),
        ],
        [wide, wide, wide_low],
        row_count,
        scans,
    )
    gated_back_low = gated_back_low.reshape(2 * row_count, lru_width)
    carry_in = carried_in(cum_coef[:, -1], lru_coef[:, 0] * local_adjoint[:, 0], True)
    carry_edge = jnp.broadcast_to(carry_in[:, None], edge[0].shape)
    branch_back, first_rows, last_rows, grad_rate, grad_input, grad_taps, grad_decay = lru_call(
        functools.partial(lru_backward_kernel, block_width),
        lru_inputs
        + [
            (cum_coef, "first"),
            (local_state, "first"),
            (start_edge, "edge"),
            (later_prod, "first"),
            (local_adjoint, "first"),
            (carry_edge, "edge"),
        ],
        [
            wide_low,
            edge,
            edge,
            (jax.ShapeDtypeStruct((lru_width, block_width), F32), "weight"),
            (jax.ShapeDtypeStruct((lru_width, block_width), F32), "weight"),
            (jax.ShapeDtypeStruct((tap_count, lru_width), F32), "taps"),
            (jax.ShapeDtypeStruct((1, lru_width), F32), "row"),
        ],
        row_count,
    )
    spill = jnp.concatenate([jnp.zeros_like(first_rows), shift_rep(first_rows, -1)], axis=1)
    for j in range(1, tap_count):
        last_rows = last_rows + conv_w[j] * spill[:, j : j + 8]
    branch_back_low = lax.dynamic_update_slice_in_dim(
        branch_back, last_rows.astype(BF16), row_count - 8, 1
    ).reshape(2 * row_count, lru_width)
    back_mix_normed = sum_parts(
        matmul_right(jnp.concatenate([branch_back_low, gated_back_low], axis=1), lru_in_w)
    )
    back_middle_norm, grad_mix_gain = jax.vjp(rms_norm, middle, gain_mix)[1](back_mix_normed)
    back_middle, down_part = lax.optimization_barrier((back_two + back_middle_norm, down_part))
    down_part = lax.psum_scatter(
        down_part, "shard", scatter_dimension=0, tiled=True, axis_index_groups=chip_groups()
    )
    grad_small = jnp.concatenate(
        [
            grad_rate.astype(BF16),
            grad_input.astype(BF16),
            grad_taps.T.astype(BF16),
            grad_decay.T.astype(BF16),
            jnp.zeros((lru_width, spare), BF16),
        ],
        axis=1,
    )

    back_one, first_grads = mlp_backward(
        resid_one, gain_first, first_in_w, first_down_w, first_kept, back_middle
    )

    attn_back_low, in_part = lax.optimization_barrier((back_one.astype(BF16), in_part))
    in_part = lax.psum_scatter(
        in_part, "shard", scatter_dimension=0, tiled=True, axis_index_groups=chip_groups()
    )
    back_halves = attn_back_low[:, : width // 2], attn_back_low[:, width // 2 :]
    back_mine, back_other = by_core(*back_halves), by_core(back_halves[1], back_halves[0])
    attended_both = with_sibling(attended_low)
    out_right = jnp.concatenate([back_mine, swap_cores(back_other)], axis=0)
    back_attended = matmul_right(back_mine, attn_own) + matmul_right(back_other, attn_sib)
    back_attended = unordered(back_attended.astype(BF16)).astype(BF16)
    back_query, back_kv_win = attention_call(
        attention_back_kernel,
        start_row,
        [query_rows, back_attended],
        kv_win,
        [
            jax.ShapeDtypeStruct((row_count, width), BF16),
            jax.ShapeDtypeStruct(kv_win.shape, F32),
        ],
    )
    back_kv = back_kv_win[behind:]
    for by in range(1, behind // row_count + 1):
        begin = behind - by * row_count
        back_kv = back_kv + shift_rep(back_kv_win[begin : begin + row_count], -by)
    back_kv = back_kv.astype(BF16)
    back_first = jnp.concatenate([back_query[:, :half], back_kv[:, :head_size]], axis=1)
    back_second = jnp.concatenate([back_query[:, half:], back_kv[:, head_size:]], axis=1)
    qkv_back_mine = by_core(back_first, back_second)
    qkv_back_other = by_core(back_second, back_first)
    back_attn_normed = matmul_right(qkv_back_mine, qkv_own) + matmul_right(qkv_back_other, qkv_sib)
    back_inputs_norm, grad_attn_gain = jax.vjp(rms_norm, inputs, gain_attn)[1](back_attn_normed)
    input_grad = (
        unordered((back_one + back_inputs_norm).astype(BF16))
        .astype(BF16)
        .reshape(1, row_count, width)
    )

    gain_given = jnp.stack([grad_attn_gain, first_grads[0], grad_mix_gain, second_grads[0]])
    gain_given = jnp.pad(gain_given, ((0, 124), (0, 0))).astype(BF16).T.reshape(reps, -1, 128)
    qkv_right = jnp.concatenate([qkv_back_mine, swap_cores(qkv_back_other)], axis=0)
    second_in = lax.all_gather(in_part, "rep", axis=0, tiled=True)
    second_down_rows = lax.all_gather(down_part, "rep", axis=0, tiled=True)
    second_in, second_down_rows, gain_given = lax.optimization_barrier(
        (second_in, second_down_rows, gain_given)
    )

    def by_reps(x):
        parts = x.reshape(chips, reps, -1, x.shape[1]).transpose(1, 0, 2, 3)
        return parts.reshape(reps, -1, x.shape[1])

    lru_in, first_in, first_down_rows, qkv_rows, out_rows, gain_rows, mix_rows, small_rows = (
        reduce_all(
            [
                (mix_normed, [branch_back_low, gated_back_low], 512),
                (first_grads[1][0], [first_grads[1][1], first_grads[2][1]], 768),
                (first_grads[3][0], [first_grads[3][1]], 512),
                (with_sibling(attn_normed), [qkv_right], 512),
                (with_sibling(attended_low), [out_right], 768),
                (None, [gain_given], 128),
                (by_reps(mix_low.T).reshape(lru_width, -1).T, [mix_back_low], 768),
                (None, [by_reps(grad_small)], 384),
            ]
        )
    )

    grad_mixer_out = unordered(mix_rows)
    small = small_rows.astype(F32)

    def in_reduced(reduced, unit, parts=1):
        return join_columns(*own_rows(reduced), 2, unit, parts)

    grad_second_gate, grad_second_up = in_reduced(second_in, ff_unit, reps)
    grad_second_down = unordered(second_down_rows)
    grad_branch_proj, grad_gated_proj = in_reduced(lru_in, lru_unit)
    grad_first_gate, grad_first_up = in_reduced(first_in, ff_unit, reps)
    grad_first_down = unordered(first_down_rows)
    qkv_mine, qkv_other = own_rows(qkv_rows)
    grad_query = jnp.concatenate(
        [by_core(qkv_mine, qkv_other)[:, :half], by_core(qkv_other, qkv_mine)[:, :half]], axis=1
    ).astype(F32)
    grad_key = by_core(qkv_mine, qkv_other)[:, half:].astype(F32)
    grad_value = by_core(qkv_other, qkv_mine)[:, half:].astype(F32)
    out_mine, out_other = own_rows(out_rows)
    grad_out_proj = unordered(
        jnp.concatenate([by_core(out_mine, out_other), by_core(out_other, out_mine)], axis=1)
    )
    gain_mine, gain_other = own_rows(gain_rows)
    gain_grads = (gain_mine.astype(F32) + gain_other.astype(F32)).T
    return (
        out_tokens,
        input_grad,
        gain_grads[0],
        grad_query,
        grad_key,
        grad_value,
        grad_out_proj,
        gain_grads[1],
        grad_first_gate,
        grad_first_up,
        grad_first_down,
        gain_grads[2],
        grad_branch_proj,
        grad_gated_proj,
        small[:, 2 * block_width : 2 * block_width + tap_count],
        small[:, :block_width],
        small[:, block_width : 2 * block_width],
        small[:, 2 * block_width + tap_count],
        grad_mixer_out,
        gain_grads[3],
        grad_second_gate,
        grad_second_up,
        grad_second_down,
    )


def solution(mesh):
    rows = P("shard", None)
    vector = P("shard")
    tokens = P("shard", "rep", None)
    weights = (
        vector,
        rows,
        rows,
        rows,
        rows,
        vector,
        rows,
        rows,
        rows,
        vector,
        rows,
        rows,
        rows,
        rows,
        rows,
        vector,
        rows,
        vector,
        rows,
        rows,
        rows,
    )
    return jax.shard_map(
        on_device,
        mesh=mesh,
        in_specs=(tokens, vector, tokens) + weights,
        out_specs=(tokens, tokens) + weights,
        check_vma=False,
    )
```

```python
import functools
import math

import jax
import jax.numpy as jnp
from jax import lax
from jax.experimental import pallas as pl
from jax.experimental.pallas import tpu as pltpu
from jax.sharding import PartitionSpec as P

WINDOW = 1024
LAG = 1
EPSILON = 1e-06
F32 = jnp.float32
BF16 = jnp.bfloat16


def rms_norm(values, norm_gain):
    return (
        values * lax.rsqrt(jnp.mean(values * values, axis=-1, keepdims=True) + EPSILON) * norm_gain
    )


def gelu_tanh(values):
    return jax.nn.gelu(values, approximate=True)


def mlp_middle(gate_pre, up_pre):
    return gelu_tanh(gate_pre) * up_pre


def matmul(first_op, second_op):
    return jnp.dot(first_op, second_op, preferred_element_type=F32)


def matmul_left(first_op, second_op):
    return lax.dot_general(
        first_op, second_op, (((0,), (0,)), ((), ())), preferred_element_type=F32
    )


def matmul_right(first_op, second_op):
    return lax.dot_general(
        first_op, second_op, (((1,), (1,)), ((), ())), preferred_element_type=F32
    )


def rounded(values):
    return values.astype(BF16).astype(F32)


def my_chip():
    return lax.axis_index("shard") // 2


def my_core():
    return lax.rem(lax.axis_index("shard"), 2)


def swap_cores(x):
    count = lax.axis_size("shard")
    return lax.ppermute(x, "shard", [(i, i ^ 1) for i in range(count)])


def shift_rep(x, by):
    size = lax.axis_size("rep")
    return lax.ppermute(x, "rep", [(i, i + by) for i in range(size) if 0 <= i + by < size])


def shift_chip(x, by):
    count = lax.axis_size("shard")
    return lax.ppermute(x, "shard", [(i, (i + 2 * by) % count) for i in range(count)])


def by_core(first, second):
    return jnp.where(my_core() == 0, first, second)


def unit_pieces(columns, unit, parts):
    sub = unit // parts
    chips = columns // unit // 2
    return sub, tuple(
        [(2 * chip + core) * unit + part * sub for part in range(parts) for chip in range(chips)]
        for core in (0, 1)
    )


def split_kernel(sub, places, core_ref, *refs):
    ins, (mine, other) = refs[:-2], refs[-2:]

    def run(core):
        for k, out in ((core, mine), (1 - core, other)):
            column = 0
            for ref in ins:
                for at in places[k]:
                    out[:, column : column + sub] = ref[:, at : at + sub]
                    column += sub

    for core in (0, 1):
        pl.when(core_ref[0] == core)(functools.partial(run, core))


def split_columns(arrays, unit, parts=1):
    sub, places = unit_pieces(arrays[0].shape[1], unit, parts)
    rows, width = arrays[0].shape
    total = width * len(arrays) // 2
    tile = 48 if rows % 48 == 0 else rows
    shape = jax.ShapeDtypeStruct((rows, total), arrays[0].dtype)
    out = pl.BlockSpec((tile, total), lambda i, core: (i, 0))
    return pl.pallas_call(
        functools.partial(split_kernel, sub, places),
        grid_spec=pltpu.PrefetchScalarGridSpec(
            num_scalar_prefetch=1,
            grid=(rows // tile,),
            in_specs=[pl.BlockSpec((tile, width), lambda i, core: (i, 0))] * len(arrays),
            out_specs=[out, out],
        ),
        out_shape=[shape, shape],
    )(my_core().astype(jnp.int32).reshape(1), *arrays)


def join_kernel(sub, places, core_ref, mine, other, *outs):
    def run(core):
        for k, ref in ((core, mine), (1 - core, other)):
            column = 0
            for out in outs:
                for at in places[k]:
                    out[:, at : at + sub] = ref[:, column : column + sub].astype(out.dtype)
                    column += sub

    for core in (0, 1):
        pl.when(core_ref[0] == core)(functools.partial(run, core))


def join_columns(mine, other, count, unit, parts=1):
    rows, total = mine.shape
    width = 2 * total // count
    sub, places = unit_pieces(width, unit, parts)
    tile = 48 if rows % 48 == 0 else rows
    half = pl.BlockSpec((tile, total), lambda i, core: (i, 0))
    return pl.pallas_call(
        functools.partial(join_kernel, sub, places),
        grid_spec=pltpu.PrefetchScalarGridSpec(
            num_scalar_prefetch=1,
            grid=(rows // tile,),
            in_specs=[half, half],
            out_specs=[pl.BlockSpec((tile, width), lambda i, core: (i, 0))] * count,
        ),
        out_shape=[jax.ShapeDtypeStruct((rows, width), F32)] * count,
    )(my_core().astype(jnp.int32).reshape(1), mine, other)


def chip_rows(mine, other):
    got = swap_cores(other)
    return jnp.concatenate([by_core(mine, got), by_core(got, mine)], axis=0)


MESH_ID = pl.DeviceIdType.MESH


def across(place, mask):
    return place + mask - 2 * mask * lax.rem(place // mask, 2)


def highest(at):
    return 1 << (at.bit_length() - 1)


def lowest(at):
    return at & -at


def gather_kernel(chunks, arrays, chips, reps, *refs):
    ins, outs = refs[:arrays], refs[arrays : 2 * arrays]
    along_send, along_recv, rep_send, rep_recv, local_sem = refs[2 * arrays :]
    shard = lax.axis_index("shard")
    chip, core = shard // 2, lax.rem(shard, 2)
    place = lax.axis_index("rep")
    bits = [1 << i for i in range(reps.bit_length() - 1)]
    everyone = range(1, reps)

    def device_at(chip_at):
        return {"shard": 2 * chip_at + core}

    barrier = pltpu.get_barrier_semaphore()
    for by in (1, chips - 1):
        pl.semaphore_signal(
            barrier,
            inc=1,
            device_id=device_at(lax.rem(chip + by, chips)),
            device_id_type=MESH_ID,
        )
    for bit in bits:
        pl.semaphore_signal(
            barrier, inc=1, device_id={"rep": across(place, bit)}, device_id_type=MESH_ID
        )
    pl.semaphore_wait(barrier, 2 + len(bits))

    def block(c, rep_at, chip_at, half=None):
        array, first, columns, sub, split = chunks[c]
        row = (rep_at * chips + chip_at) * sub if split else chip_at * sub
        if half is not None:
            columns = columns // 2
            first = first + half * columns
        return outs[array].at[pl.ds(pl.multiple_of(row, 16), sub), pl.ds(first, columns)]

    def own(c):
        array, first, columns, sub, split = chunks[c]
        row = pl.multiple_of(place * sub, 16) if split else 0
        return ins[array].at[pl.ds(row, sub), pl.ds(first, columns)]

    def along(c, origin, to, direction):
        here = block(c, place, origin)
        return here, pltpu.make_async_remote_copy(
            src_ref=here,
            dst_ref=here,
            send_sem=along_send.at[c, origin, direction],
            recv_sem=along_recv.at[c, origin],
            device_id=device_at(to),
            device_id_type=MESH_ID,
        )

    def first_along(c, to, direction):
        return pltpu.make_async_remote_copy(
            src_ref=own(c),
            dst_ref=block(c, place, chip),
            send_sem=along_send.at[c, chip, direction],
            recv_sem=along_recv.at[c, chip],
            device_id=device_at(to),
            device_id_type=MESH_ID,
        )

    def hop(c, chip_at, at, half):
        bit = at if half is None else (highest(at) if half == 0 else lowest(at))
        here = block(c, across_all(place, at ^ bit), chip_at, half)
        slot = 2 * at + (half or 0)
        return pltpu.make_async_remote_copy(
            src_ref=here,
            dst_ref=here,
            send_sem=rep_send.at[c, chip_at, slot],
            recv_sem=rep_recv.at[c, chip_at, slot],
            device_id={"rep": across(place, bit)},
            device_id_type=MESH_ID,
        )

    def arrival(c, chip_at, at, half):
        here = block(c, across_all(place, at), chip_at, half)
        slot = 2 * at + (half or 0)
        return pltpu.make_async_remote_copy(
            src_ref=here,
            dst_ref=here,
            send_sem=rep_send.at[c, chip_at, slot],
            recv_sem=rep_recv.at[c, chip_at, slot],
            device_id={"rep": place},
            device_id_type=MESH_ID,
        )

    def across_all(at, offset):
        for bit in bits:
            if offset & bit:
                at = across(at, bit)
        return at

    def halves(at):
        return (None,) if at == lowest(at) else (0, 1)

    def local_copies(c):
        array, first, columns, sub, split = chunks[c]
        copies = []
        for part in range(reps if split else 1):
            copies.append(
                pltpu.make_async_copy(
                    ins[array].at[pl.ds(part * sub, sub), pl.ds(first, columns)],
                    block(c, part, chip),
                    local_sem.at[c, part],
                )
            )
        return copies

    def others(run):
        def one(by, carry):
            run(lax.rem(chip + by, chips))
            return carry

        lax.fori_loop(1, chips, one, 0)

    def begin(c):
        @pl.when(chip < chips - 1)
        def _():
            first_along(c, chip + 1, 0).start()

        @pl.when(chip > 0)
        def _():
            first_along(c, chip - 1, 1).start()

        for copy in local_copies(c):
            copy.start()

    def spread(c, origin):
        if chunks[c][4]:
            for bit in bits:
                hop(c, origin, bit, None).start()

    def arrived(c, by):
        @pl.when(chip - by >= 0)
        def _():
            along(c, chip - by, chip, 0)[1].wait_recv()

            @pl.when(chip < chips - 1)
            def _():
                along(c, chip - by, chip + 1, 0)[1].start()

            spread(c, chip - by)

        @pl.when(chip + by < chips)
        def _():
            along(c, chip + by, chip, 1)[1].wait_recv()

            @pl.when(chip > 0)
            def _():
                along(c, chip + by, chip - 1, 1)[1].start()

            spread(c, chip + by)

    def passed(c, level):
        if not chunks[c][4]:
            return

        def run(origin):
            for at in everyone:
                if at.bit_count() == level:
                    for half in halves(at):
                        arrival(c, origin, at, half).wait_recv()
            for at in everyone:
                if at.bit_count() == level + 1:
                    for half in halves(at):
                        hop(c, origin, at, half).start()

        others(run)

    def end(c):
        @pl.when(chip < chips - 1)
        def _():
            first_along(c, chip + 1, 0).wait_send()

        @pl.when(chip > 0)
        def _():
            first_along(c, chip - 1, 1).wait_send()

        for copy in local_copies(c):
            copy.wait()
        for by in range(1, chips):

            @pl.when((chip - by >= 0) & (chip < chips - 1))
            def _(by=by):
                along(c, chip - by, chip + 1, 0)[1].wait_send()

            @pl.when((chip + by < chips) & (chip > 0))
            def _(by=by):
                along(c, chip + by, chip - 1, 1)[1].wait_send()

        if chunks[c][4]:

            def run(origin):
                for at in everyone:
                    for half in halves(at):
                        hop(c, origin, at, half).wait_send()

            others(run)

    stages = (
        [begin]
        + [functools.partial(arrived, by=by) for by in range(1, chips)]
        + [functools.partial(passed, level=level) for level in range(1, len(bits) + 1)]
        + [end]
    )
    for tick in range(len(chunks) + (len(stages) - 1) * LAG):
        for at, stage in enumerate(stages):
            if 0 <= tick - at * LAG < len(chunks):
                stage(tick - at * LAG)


def chip_groups():
    count = lax.axis_size("shard")
    return [list(range(core, count, 2)) for core in (0, 1)]


def gather_plain(array, split):
    if split:
        part = array.shape[0] // lax.axis_size("rep")
        array = lax.dynamic_slice_in_dim(array, lax.axis_index("rep") * part, part, 0)
    array = lax.all_gather(array, "shard", axis=0, tiled=True, axis_index_groups=chip_groups())
    return lax.all_gather(array, "rep", axis=0, tiled=True) if split else array


def reduce_plain(whole):
    part = lax.psum_scatter(whole, "rep", scatter_dimension=0, tiled=True)
    part = lax.psum_scatter(
        part, "shard", scatter_dimension=0, tiled=True, axis_index_groups=chip_groups()
    )
    return lax.all_gather(part, "rep", axis=0, tiled=True)


def gather_all(arrays, splits, widths):
    reps, chips = lax.axis_size("rep"), lax.axis_size("shard") // 2
    if any(split and array.shape[0] // reps % 16 for array, split in zip(arrays, splits)):
        return [gather_plain(array, split) for array, split in zip(arrays, splits)]
    chunks = []
    for i, (array, split, wide) in enumerate(zip(arrays, splits, widths)):
        sub = array.shape[0] // reps if split else array.shape[0]
        for first in range(0, array.shape[1], wide):
            chunks.append((i, first, min(wide, array.shape[1] - first), sub, split))
    slots = 2 * reps
    count = len(chunks)
    return pl.pallas_call(
        functools.partial(gather_kernel, chunks, len(arrays), chips, reps),
        in_specs=[pl.BlockSpec(memory_space=pltpu.VMEM)] * len(arrays),
        out_specs=[pl.BlockSpec(memory_space=pl.ANY)] * len(arrays),
        out_shape=[
            jax.ShapeDtypeStruct((a.shape[0] * chips, a.shape[1]), a.dtype) for a in arrays
        ],
        scratch_shapes=[
            pltpu.SemaphoreType.DMA((count, chips, 2)),
            pltpu.SemaphoreType.DMA((count, chips)),
            pltpu.SemaphoreType.DMA((count, chips, slots)),
            pltpu.SemaphoreType.DMA((count, chips, slots)),
            pltpu.SemaphoreType.DMA((count, reps)),
        ],
        compiler_params=pltpu.CompilerParams(
            collective_id=0, has_side_effects=True, vmem_limit_bytes=40 * 1024 * 1024
        ),
        cost_estimate=pl.CostEstimate(
            flops=0, bytes_accessed=sum(70 * a.size for a in arrays), transcendentals=0
        ),
    )(*arrays)


def reduce_kernel(chunks, counts, chips, *refs):
    n_left, n_right, n_given, n_out = counts
    n = len(chunks)
    refs = list(refs)

    def take(count):
        taken = refs[:count]
        del refs[:count]
        return taken

    lefts, rights, givens = take(n_left), take(n_right), take(n_given)
    outs, first_in, second_in, chip_in = take(n_out), take(n), take(n), take(n)
    right_buf, big_left, first_out, first_loc, second_out, second_loc = take(6)
    chip_out, chip_loc, own_out = take(3)
    send, recv, chip_send, chip_recv, hop_send, hop_recv, local = take(7)
    shard = lax.axis_index("shard")
    chip, core = shard // 2, lax.rem(shard, 2)
    place = lax.axis_index("rep")
    bits = (1, 2)

    def device_at(chip_at):
        return {"shard": 2 * chip_at + core}

    barrier = pltpu.get_barrier_semaphore()
    for by in range(1, chips):
        pl.semaphore_signal(
            barrier,
            inc=1,
            device_id=device_at(lax.rem(chip + by, chips)),
            device_id_type=MESH_ID,
        )
    for bit in bits:
        pl.semaphore_signal(
            barrier, inc=1, device_id={"rep": across(place, bit)}, device_id_type=MESH_ID
        )
    pl.semaphore_wait(barrier, chips - 1 + len(bits))

    def rep_at(offset):
        at = place
        for bit in bits:
            if offset & bit:
                at = across(at, bit)
        return at

    def masks(c):
        return bits[::-1] if chunks[c]["flip"] else bits

    def rows_of(c):
        return chips * chunks[c]["sub"]

    def right_copy(c):
        k = chunks[c]
        return pltpu.make_async_copy(
            rights[k["right"]].at[:, pl.ds(k["first"], k["wide"])],
            right_buf.at[c % 8, :, pl.ds(0, k["wide"])],
            local.at[c, 0],
        )

    def left_copy(c):
        return pltpu.make_async_copy(lefts[chunks[c]["left"]], big_left, local.at[c, 1])

    def exchange(c, turn):
        k, rows = chunks[c], rows_of(c)
        source, target = ((first_out, first_in), (second_out, second_in))[turn]
        return pltpu.make_async_remote_copy(
            src_ref=source.at[c % 4, :, pl.ds(0, rows), pl.ds(0, k["wide"])],
            dst_ref=target[c],
            send_sem=send.at[c, turn],
            recv_sem=recv.at[c, turn],
            device_id={"rep": across(place, masks(c)[turn])},
            device_id_type=MESH_ID,
        )

    def arrived_copy(c, turn):
        k, rows = chunks[c], rows_of(c)
        source = (first_in, second_in)[turn][c]
        target = (first_loc.at[c % 5], second_loc.at[c % 2])[turn]
        return pltpu.make_async_copy(
            source, target.at[:, pl.ds(0, rows), pl.ds(0, k["wide"])], local.at[c, 2 + turn]
        )

    def tiles(c, run):
        wide = chunks[c]["wide"]
        tile = 256 if wide % 256 == 0 else 128

        def one(i, carry):
            run(pl.ds(pl.multiple_of(i * tile, tile), tile))
            return carry

        lax.fori_loop(0, wide // tile, one, 0)

    def product(c, offset, target, arrivals):
        k, rows = chunks[c], rows_of(c)
        at = rep_at(offset)

        def run(columns):
            if k["given"] is not None:
                total = givens[k["given"]][at, :, columns].astype(F32)
            else:
                right = right_buf[c % 8, :, columns]
                if k["big"]:
                    total = jnp.dot(big_left[at], right, preferred_element_type=F32)
                else:
                    left = lefts[k["left"]][:, pl.ds(pl.multiple_of(at * rows, 128), rows)]
                    total = matmul_left(left, right)
            for ref, index in arrivals:
                total = total + ref[index + (pl.ds(0, rows), columns)].astype(F32)
            target[0][target[1] + (pl.ds(0, rows), columns)] = total.astype(BF16)

        tiles(c, run)

    def load(c):
        if chunks[c]["given"] is None:
            right_copy(c).start()
            if chunks[c]["load"]:
                left_copy(c).start()

    def send_first(c):
        if chunks[c]["given"] is None:
            right_copy(c).wait()
            if chunks[c]["load"]:
                left_copy(c).wait()
        one, two = masks(c)
        product(c, one, (first_out, (c % 4, 0)), [])
        product(c, one ^ two, (first_out, (c % 4, 1)), [])
        exchange(c, 0).start()

    def take_first(c):
        exchange(c, 0).wait_recv()
        arrived_copy(c, 0).start()

    def send_second(c):
        arrived_copy(c, 0).wait()
        product(c, masks(c)[1], (second_out, (c % 4, 0)), [(first_loc, (c % 5, 1))])
        exchange(c, 1).start()
        exchange(c, 0).wait_send()

    def take_second(c):
        exchange(c, 1).wait_recv()
        arrived_copy(c, 1).start()

    def to_chip(c, by):
        k = chunks[c]
        at = lax.rem(chip + by, chips)
        row = pl.multiple_of(at * k["sub"], 16)
        return pltpu.make_async_remote_copy(
            src_ref=chip_out.at[c % 3, pl.ds(row, k["sub"]), pl.ds(0, k["wide"])],
            dst_ref=chip_in[c].at[by - 1],
            send_sem=chip_send.at[c, by - 1],
            recv_sem=chip_recv.at[c, by - 1],
            device_id=device_at(at),
            device_id_type=MESH_ID,
        )

    def send_chips(c):
        arrived_copy(c, 1).wait()
        product(
            c, 0, (chip_out, (c % 3,)), [(first_loc, (c % 5, 0)), (second_loc, (c % 2, 0))]
        )
        for by in range(1, chips):
            to_chip(c, by).start()
        exchange(c, 1).wait_send()

    def chips_copy(c):
        k = chunks[c]
        return pltpu.make_async_copy(
            chip_in[c],
            chip_loc.at[c % 2, :, pl.ds(0, k["sub"]), pl.ds(0, k["wide"])],
            local.at[c, 4],
        )

    def take_chips(c):
        for by in range(1, chips):
            to_chip(c, by).wait_recv()
        chips_copy(c).start()

    def out_rows(c, offset, half=None):
        k = chunks[c]
        first, wide = k["place"], k["wide"]
        if half is not None:
            wide = wide // 2
            first = first + half * wide
        row = pl.multiple_of(rep_at(offset) * k["sub"], 16)
        return outs[k["out"]].at[pl.ds(row, k["sub"]), pl.ds(first, wide)]

    def own_rows_of(c):
        k = chunks[c]
        return own_out.at[c % 3, pl.ds(0, k["sub"]), pl.ds(0, k["wide"])]

    def own_copy(c):
        return pltpu.make_async_copy(own_rows_of(c), out_rows(c, 0), local.at[c, 5])

    def hop(c, at, half):
        bit = at if at in bits else (2 if half != 1 else 1)
        here = out_rows(c, at ^ bit, half)
        slot = 2 * at + (half or 0)
        return pltpu.make_async_remote_copy(
            src_ref=own_rows_of(c) if at in bits else here,
            dst_ref=here,
            send_sem=hop_send.at[c, slot],
            recv_sem=hop_recv.at[c, slot],
            device_id={"rep": across(place, bit)},
            device_id_type=MESH_ID,
        )

    def arrival(c, at, half):
        here = out_rows(c, at, half)
        slot = 2 * at + (half or 0)
        return pltpu.make_async_remote_copy(
            src_ref=here,
            dst_ref=here,
            send_sem=hop_send.at[c, slot],
            recv_sem=hop_recv.at[c, slot],
            device_id={"rep": across(place, 1)},
            device_id_type=MESH_ID,
        )

    def far_halves(c):
        return (0, 1) if chunks[c]["wide"] % 256 == 0 else (None,)

    def send_sums(c):
        k = chunks[c]
        chips_copy(c).wait()
        row = pl.multiple_of(chip * k["sub"], 16)

        def run(columns):
            total = chip_out[c % 3, pl.ds(row, k["sub"]), columns].astype(F32)
            for by in range(1, chips):
                total = total + chip_loc[c % 2, by - 1, pl.ds(0, k["sub"]), columns].astype(F32)
            own_out[c % 3, pl.ds(0, k["sub"]), columns] = total.astype(BF16)

        tiles(c, run)
        for bit in bits:
            hop(c, bit, None).start()
        own_copy(c).start()
        for by in range(1, chips):
            to_chip(c, by).wait_send()

    def pass_sums(c):
        for bit in bits:
            arrival(c, bit, None).wait_recv()
        for half in far_halves(c):
            hop(c, 3, half).start()

    def end(c):
        own_copy(c).wait()
        for bit in bits:
            hop(c, bit, None).wait_send()
        for half in far_halves(c):
            arrival(c, 3, half).wait_recv()
            hop(c, 3, half).wait_send()

    stages = [
        load,
        send_first,
        None,
        take_first,
        send_second,
        None,
        take_second,
        send_chips,
        take_chips,
        send_sums,
        pass_sums,
        end,
    ]
    for tick in range(n + len(stages) - 1):
        for at, stage in enumerate(stages):
            if stage is not None and 0 <= tick - at < n:
                stage(tick - at)


def reduce_all(products):
    reps, chips = lax.axis_size("rep"), lax.axis_size("shard") // 2
    depth = max(left.shape[0] for left, _, _ in products if left is not None)
    if reps != 4 or any(
        (given[0].shape[1] if left is None else left.shape[1] // reps) // chips % 16
        for left, given, _ in products
    ):
        results = []
        for left, given, _ in products:
            if left is None:
                whole = given[0].reshape(-1, given[0].shape[2])
            else:
                whole = jnp.concatenate(
                    [matmul_left(left, right).astype(BF16) for right in given], axis=1
                )
            results.append(reduce_plain(whole))
        return results
    lefts, rights, givens, chunks, outs = [], [], [], [], []
    subs = [
        (given[0].shape[1] if left is None else left.shape[1] // reps) // chips
        for left, given, _ in products
    ]
    largest = max(subs)
    for (left, parts, wide), sub in zip(products, subs):
        total = sum(part.shape[-1] for part in parts)
        outs.append(jax.ShapeDtypeStruct((reps * sub, total), BF16))
        first_right = len(rights)
        if left is not None:
            lefts.append(left.T.reshape(reps, chips * sub, depth) if sub == largest else left)
            rights.extend(parts)
        else:
            givens.extend(parts)
        before = 0
        mine = []
        for i, part in enumerate(parts):
            row = []
            for first in range(0, part.shape[-1], wide):
                row.append(
                    dict(
                        left=len(lefts) - 1,
                        given=len(givens) - 1 if left is None else None,
                        right=first_right + i,
                        first=first,
                        wide=min(wide, part.shape[-1] - first),
                        sub=sub,
                        out=len(outs) - 1,
                        place=before + first,
                        big=sub == largest,
                        load=False,
                    )
                )
            mine.append(row)
            before += part.shape[-1]
        mine = [chunk for group in zip(*mine) for chunk in group]
        mine[0]["load"] = sub == largest
        chunks += mine
    for i, chunk in enumerate(chunks):
        chunk["flip"] = i % 2
    n = len(chunks)
    rows = max(subs) * chips
    wide = max(chunk["wide"] for chunk in chunks)
    hbm = pl.BlockSpec(memory_space=pl.ANY)
    vmem = pl.BlockSpec(memory_space=pltpu.VMEM)
    big = {chunk["left"] for chunk in chunks if chunk["big"]}

    def landing(blocks, sub_only=False):
        return [
            jax.ShapeDtypeStruct(
                (blocks, c["sub"] if sub_only else chips * c["sub"], c["wide"]), BF16
            )
            for c in chunks
        ]

    shapes = outs + landing(2) + landing(1) + landing(chips - 1, True)
    results = pl.pallas_call(
        functools.partial(
            reduce_kernel, chunks, (len(lefts), len(rights), len(givens), len(outs)), chips
        ),
        in_specs=[hbm if i in big else vmem for i in range(len(lefts))]
        + [hbm] * len(rights)
        + [vmem] * len(givens),
        out_specs=[hbm] * len(shapes),
        out_shape=shapes,
        scratch_shapes=[
            pltpu.VMEM((8, depth, wide), BF16),
            pltpu.VMEM((reps, rows, depth), BF16),
            pltpu.VMEM((4, 2, rows, wide), BF16),
            pltpu.VMEM((5, 2, rows, wide), BF16),
            pltpu.VMEM((4, 1, rows, wide), BF16),
            pltpu.VMEM((2, 1, rows, wide), BF16),
            pltpu.VMEM((3, rows, wide), BF16),
            pltpu.VMEM((2, chips - 1, max(subs), wide), BF16),
            pltpu.VMEM((3, max(subs), wide), BF16),
            pltpu.SemaphoreType.DMA((n, 2)),
            pltpu.SemaphoreType.DMA((n, 2)),
            pltpu.SemaphoreType.DMA((n, chips - 1)),
            pltpu.SemaphoreType.DMA((n, chips - 1)),
            pltpu.SemaphoreType.DMA((n, 8)),
            pltpu.SemaphoreType.DMA((n, 8)),
            pltpu.SemaphoreType.DMA((n, 6)),
        ],
        compiler_params=pltpu.CompilerParams(
            collective_id=1, has_side_effects=True, vmem_limit_bytes=62 * 1024 * 1024
        ),
        cost_estimate=pl.CostEstimate(
            flops=0,
            bytes_accessed=sum(128 * shape.size for shape in outs),
            transcendentals=0,
        ),
    )(*lefts, *rights, *givens)
    return results[: len(outs)]


def own_rows(rows):
    part = rows.shape[0] // 2
    core = my_core()
    mine = lax.dynamic_slice_in_dim(rows, core * part, part, 0)
    return mine, swap_cores(lax.dynamic_slice_in_dim(rows, (1 - core) * part, part, 0))


ROOT = math.sqrt(2.0 / math.pi)


def gelu_parts(v):
    inner = jnp.tanh(ROOT * (v + 0.044715 * v * v * v))
    value = 0.5 * v * (1.0 + inner)
    slope = 0.5 * (1.0 + inner) + 0.5 * v * (1.0 - inner * inner) * ROOT * (
        1.0 + 3.0 * 0.044715 * v * v
    )
    return value, slope


def one_minus_exp(v):
    series = 1.0 + v / 8.0
    for order in (7.0, 6.0, 5.0, 4.0, 3.0, 2.0):
        series = 1.0 + v * series * (1.0 / order)
    return -v * series


def sigmoid(v):
    return 1.0 / (1.0 + jnp.exp(-v))


def scan_rows(a, b, a_ref, b_ref, cum_ref, out_ref, reverse):
    rows, lanes = a.shape
    place = lax.rem(lax.broadcasted_iota(jnp.int32, (rows, lanes), 0), 8)
    for k in (1, 2, 4):
        by = rows - k if reverse else k
        inside = place < 8 - k if reverse else place >= k
        a_before = jnp.where(inside, pltpu.roll(a, by, 0), 1.0)
        b_before = jnp.where(inside, pltpu.roll(b, by, 0), 0.0)
        b = a * b_before + b
        a = a * a_before
    a_ref[...] = a
    b_ref[...] = b
    groups = rows // 8
    last = 0 if reverse else 7

    def step(turn, carry):
        carry_cum, carry_out = carry
        group = groups - 1 - turn if reverse else turn
        where = pl.ds(pl.multiple_of(group * 8, 8), 8)
        out = b_ref[where, :] + a_ref[where, :] * carry_out
        cum = a_ref[where, :] * carry_cum
        out_ref[0, where, :] = out
        cum_ref[0, where, :] = cum
        return (
            jnp.broadcast_to(cum[last : last + 1], (8, lanes)),
            jnp.broadcast_to(out[last : last + 1], (8, lanes)),
        )

    lax.fori_loop(
        0, groups, step, (jnp.ones((8, lanes), F32), jnp.zeros((8, lanes), F32)), unroll=4
    )


def shifted_rows(x, tail, by):
    return pltpu.roll(jnp.concatenate([tail, x], axis=0), by, 0)[8:] if by else x


def conv_rows(branch, tail, taps):
    return sum(taps[j : j + 1] * shifted_rows(branch, tail, j) for j in range(taps.shape[0]))


def by_blocks(low, weights, block, contract=0):
    parts = []
    for i in range(low.shape[1] // block):
        parts.append(
            lax.dot_general(
                low[:, i * block : (i + 1) * block],
                weights[i * block : (i + 1) * block],
                (((1,), (contract,)), ((), ())),
                preferred_element_type=F32,
            )
        )
    return jnp.concatenate(parts, axis=1)


def lru_forward_kernel(
    block, branch_ref, tail_ref, rate_ref, input_ref, taps_ref, decay_ref,
    coef_ref, cum_ref, state_ref, cum_last_ref, state_last_ref, a_ref, b_ref,
):
    conv = conv_rows(branch_ref[0], tail_ref[0], taps_ref[...])
    low = conv.astype(BF16)
    log_coef = -8.0 * sigmoid(by_blocks(low, rate_ref[...], block)) * decay_ref[...]
    coef = jnp.exp(log_coef)
    gate = sigmoid(by_blocks(low, input_ref[...], block))
    drive = jnp.sqrt(one_minus_exp(2.0 * log_coef)) * gate * conv
    coef_ref[0] = coef
    scan_rows(coef, drive, a_ref, b_ref, cum_ref, state_ref, False)
    rows = coef.shape[0]
    cum_last_ref[0] = cum_ref[0, rows - 8 :, :]
    state_last_ref[0] = state_ref[0, rows - 8 :, :]


def lru_adjoint_kernel(
    gated_ref, coef_ref, cum_ref, local_ref, start_ref, back_ref,
    later_ref, adjoint_ref, gated_back_ref, first_ref, a_ref, b_ref,
):
    value, slope = gelu_parts(gated_ref[0])
    back = back_ref[0].astype(F32)
    state = local_ref[0] + cum_ref[0] * start_ref[0][:1]
    gated_back_ref[0] = (back * state * slope).astype(BF16)
    coef = coef_ref[0]
    rows = coef.shape[0]
    last = lax.broadcasted_iota(jnp.int32, coef.shape, 0) == rows - 1
    coef_next = jnp.where(last, 1.0, pltpu.roll(coef, rows - 1, 0))
    scan_rows(coef_next, back * value, a_ref, b_ref, later_ref, adjoint_ref, True)
    first_ref[0] = coef[:8] * adjoint_ref[0, :8, :]


def lru_backward_kernel(
    block, branch_ref, tail_ref, rate_ref, input_ref, taps_ref, decay_ref,
    cum_ref, local_ref, start_ref, later_ref, adjoint_ref, carry_ref,
    branch_back_ref, first_ref, last_ref, rate_grad_ref, input_grad_ref, taps_grad_ref, decay_grad_ref,
):
    branch, tail, taps, decay = branch_ref[0], tail_ref[0], taps_ref[...], decay_ref[...]
    rows = branch.shape[0]
    conv = conv_rows(branch, tail, taps)
    low = conv.astype(BF16)
    rate = sigmoid(by_blocks(low, rate_ref[...], block))
    gate = sigmoid(by_blocks(low, input_ref[...], block))
    log_coef = -8.0 * rate * decay
    coef = jnp.exp(log_coef)
    root = jnp.sqrt(one_minus_exp(2.0 * log_coef))
    start = start_ref[0][:1]
    state = local_ref[0] + cum_ref[0] * start
    first = lax.broadcasted_iota(jnp.int32, state.shape, 0) == 0
    before = jnp.where(first, start, pltpu.roll(state, 1, 0))
    adjoint = adjoint_ref[0] + later_ref[0] * carry_ref[0][:1]
    back_root = adjoint * gate * conv
    back_log = (adjoint * before - back_root * coef / root) * coef
    back_rate = back_log * (-8.0 * decay) * rate * (1.0 - rate)
    back_gate = adjoint * root * conv * gate * (1.0 - gate)
    rate_low, gate_low = back_rate.astype(BF16), back_gate.astype(BF16)
    back_conv = (
        adjoint * root * gate
        + by_blocks(rate_low, rate_ref[...], block, 1)
        + by_blocks(gate_low, input_ref[...], block, 1)
    )

    def block_grads(back):
        return jnp.concatenate(
            [
                lax.dot_general(
                    low[:, i : i + block],
                    back[:, i : i + block],
                    (((0,), (0,)), ((), ())),
                    preferred_element_type=F32,
                )
                for i in range(0, low.shape[1], block)
            ],
            axis=0,
        )

    taps_grad = jnp.concatenate(
        [
            jnp.sum(back_conv * shifted_rows(branch, tail, j), axis=0, keepdims=True)
            for j in range(taps.shape[0])
        ],
        axis=0,
    )
    grads = (
        (rate_grad_ref, block_grads(rate_low)),
        (input_grad_ref, block_grads(gate_low)),
        (taps_grad_ref, taps_grad),
        (decay_grad_ref, jnp.sum(back_log * (-8.0 * rate), axis=0, keepdims=True)),
    )

    @pl.when(pl.program_id(1) == 0)
    def _():
        for ref, grad in grads:
            ref[...] = grad

    @pl.when(pl.program_id(1) > 0)
    def _():
        for ref, grad in grads:
            ref[...] += grad

    extended = jnp.concatenate([back_conv, jnp.zeros((8, branch.shape[1]), F32)], axis=0)
    branch_back = sum(
        taps[j : j + 1] * (pltpu.roll(extended, rows + 8 - j, 0)[:rows] if j else back_conv)
        for j in range(taps.shape[0])
    )
    branch_back_ref[0] = branch_back.astype(BF16)
    first_ref[0] = back_conv[:8]
    last_ref[0] = branch_back[rows - 8 :]


def lru_call(kernel, arrays, outs, rows, scratch=()):
    lanes = 256
    kinds = {
        "first": ((1, rows, lanes), lambda i, b: (b, 0, i)),
        "second": ((1, rows, lanes), None),
        "edge": ((1, 8, lanes), lambda i, b: (b, 0, i)),
        "weight": ((lanes, 128), lambda i, b: (i, 0)),
        "taps": ((4, lanes), lambda i, b: (0, i)),
        "row": ((1, lanes), lambda i, b: (0, i)),
    }
    width = max(a.shape[-1] for a, kind in outs if kind == "first")

    def spec(kind):
        shape, place = kinds[kind]
        if kind == "second":
            place = lambda i, b: (b, 0, i + width // lanes)
        return pl.BlockSpec(shape, place)

    return pl.pallas_call(
        kernel,
        grid=(width // lanes, 2),
        in_specs=[spec(kind) for _, kind in arrays],
        out_specs=[spec(kind) for _, kind in outs],
        out_shape=[a for a, _ in outs],
        scratch_shapes=list(scratch),
        compiler_params=pltpu.CompilerParams(vmem_limit_bytes=56 * 1024 * 1024),
        cost_estimate=pl.CostEstimate(
            flops=0, bytes_accessed=16 * rows * width * 4, transcendentals=0
        ),
    )(*[a for a, _ in arrays])


def carried_in(prod, part, reverse):
    size = lax.axis_size("rep")
    pair = jnp.stack([prod, part])
    total = jnp.zeros_like(part)
    through = jnp.ones_like(prod)
    place = lax.axis_index("rep")
    ahead = size - 1 - place if reverse else place
    for distance in range(1, size):
        got = shift_rep(pair, -distance if reverse else distance)
        total = total + through * got[1]
        through = jnp.where(ahead >= distance, through * got[0], through)
    return total


def block_probs(query, keys, lowest):
    scores = lax.dot_general(
        query, keys, (((1,), (1,)), ((), ())), preferred_element_type=F32
    ) * (1.0 / math.sqrt(query.shape[1]))
    row = lax.broadcasted_iota(jnp.int32, scores.shape, 0)
    column = lax.broadcasted_iota(jnp.int32, scores.shape, 1)
    allowed = (column > row) & (column <= row + WINDOW) & (column >= lowest)
    scores = jnp.where(allowed, scores, -1e30)
    powers = jnp.exp(scores - jnp.max(scores, axis=1, keepdims=True))
    return powers * (1.0 / jnp.sum(powers, axis=1, keepdims=True))


def attention_kernel(start_ref, query_ref, kv_ref, out_ref):
    rows, size = query_ref.shape
    block = min(256, rows)
    for first in range(0, rows, block):
        keys = kv_ref[first : first + block + WINDOW, :size]
        values = kv_ref[first : first + block + WINDOW, size:]
        probs = block_probs(
            query_ref[first : first + block, :], keys, WINDOW - first - start_ref[0]
        )
        out_ref[first : first + block, :] = jnp.dot(
            probs.astype(BF16), values, preferred_element_type=F32
        ).astype(BF16)


def attention_back_kernel(start_ref, query_ref, back_ref, kv_ref, query_back_ref, kv_back_ref):
    rows, size = query_ref.shape
    block = min(256, rows)
    scale = 1.0 / math.sqrt(size)

    @pl.when(pl.program_id(0) == 0)
    def _():
        kv_back_ref[...] = jnp.zeros_like(kv_back_ref)

    for first in range(0, rows, block):
        here = slice(first, first + block + WINDOW)
        keys, values = kv_ref[here, :size], kv_ref[here, size:]
        query = query_ref[first : first + block, :]
        back = back_ref[first : first + block, :]
        probs = block_probs(query, keys, WINDOW - first - start_ref[0])
        back_probs = lax.dot_general(
            back, values, (((1,), (1,)), ((), ())), preferred_element_type=F32
        )
        prob_dot = jnp.sum(probs * back_probs, axis=1, keepdims=True)
        back_scores = (probs * (back_probs - prob_dot)).astype(BF16)
        query_back_ref[first : first + block, :] = (
            jnp.dot(back_scores, keys, preferred_element_type=F32) * scale
        ).astype(BF16)
        kv_back_ref[here, :size] += (
            lax.dot_general(
                back_scores, query, (((0,), (0,)), ((), ())), preferred_element_type=F32
            )
            * scale
        )
        kv_back_ref[here, size:] += lax.dot_general(
            probs.astype(BF16), back, (((0,), (0,)), ((), ())), preferred_element_type=F32
        )


def attention_call(kernel, start, by_head, kv, outs):
    rows, width = by_head[0].shape
    size = kv.shape[1] // 2
    head = pl.BlockSpec((rows, size), lambda h, start: (0, h))
    whole = pl.BlockSpec(kv.shape, lambda h, start: (0, 0))
    return pl.pallas_call(
        kernel,
        grid_spec=pltpu.PrefetchScalarGridSpec(
            num_scalar_prefetch=1,
            grid=(width // size,),
            in_specs=[head] * len(by_head) + [whole],
            out_specs=[head, whole][: len(outs)],
        ),
        out_shape=outs,
        compiler_params=pltpu.CompilerParams(vmem_limit_bytes=56 * 1024 * 1024),
        cost_estimate=pl.CostEstimate(
            flops=12 * rows * width * WINDOW,
            bytes_accessed=64 * 1024 * 1024,
            transcendentals=0,
        ),
    )(jnp.reshape(start, (1,)), *by_head, kv)


def with_sibling(x):
    return jnp.concatenate([x, swap_cores(x)], axis=0)


def sum_parts(parts):
    rows = parts.shape[0] // 2
    return parts[:rows] + swap_cores(parts[rows:])


def mlp_forward(resid, norm_gain, in_w, down_w):
    normed = with_sibling(rms_norm(resid, norm_gain).astype(BF16))
    middle = in_w.shape[1] // 2
    both = matmul(normed, in_w)
    gate_pre, up_pre = both[:, :middle], both[:, middle:]
    hidden = mlp_middle(gate_pre, up_pre).astype(BF16)
    return resid + sum_parts(matmul(hidden, down_w)), (normed, gate_pre, up_pre, hidden)


def mlp_backward(resid, norm_gain, in_w, down_w, kept_vals, back_out):
    normed, gate_pre, up_pre, hidden = kept_vals
    out_low = with_sibling(back_out.astype(BF16))
    back_hidden = rounded(matmul_right(out_low, down_w))
    back_gate, back_up = jax.vjp(mlp_middle, gate_pre, up_pre)[1](back_hidden)
    gate_low = back_gate.astype(BF16)
    up_low = back_up.astype(BF16)
    back_normed = sum_parts(matmul_right(jnp.concatenate([gate_low, up_low], axis=1), in_w))
    back_resid, grad_gain = jax.vjp(rms_norm, resid, norm_gain)[1](back_normed)
    return (back_out + back_resid, (grad_gain, (normed, gate_low), (normed, up_low), (hidden, out_low)))


def on_device(
    tokens_in,
    lengths,
    cotangent,
    attn_norm,
    query_proj,
    key_proj,
    value_proj,
    attn_out,
    first_norm,
    first_gate,
    first_up,
    first_down,
    mixer_norm,
    branch_proj,
    gated_proj,
    conv_taps,
    rate_gate,
    input_gate,
    decay_rate,
    mixer_out,
    second_norm,
    second_gate,
    second_up,
    second_down,
):
    row_count = tokens_in.shape[1]
    width = tokens_in.shape[2]
    shards = lax.axis_size("shard")
    reps = lax.axis_size("rep")
    chips = shards // 2
    core = my_core()
    start_row = lax.axis_index("rep") * row_count
    positions = start_row + jnp.arange(row_count, dtype=jnp.int32)
    valid_mask = (positions < lengths[0]).astype(F32)[:, None]

    piece = width // chips // reps
    spot = lax.broadcasted_iota(jnp.int32, (width, width), 1)
    natural = (
        lax.rem(spot // piece, chips) * (piece * reps)
        + (spot // (piece * chips)) * piece
        + lax.rem(spot, piece)
    )
    to_order = (lax.broadcasted_iota(jnp.int32, (width, width), 0) == natural).astype(BF16)

    def ordered(x):
        return matmul(x, to_order)

    def unordered(x):
        return matmul_right(x, to_order)

    head_size = key_proj.shape[1]
    half = query_proj.shape[1] // 2
    gain_columns = jnp.stack([attn_norm, first_norm, mixer_norm, second_norm], axis=1)
    gain_columns = jnp.pad(gain_columns, ((0, 0), (0, 128 - 4)))
    qkv_halves = (
        jnp.concatenate([query_proj[:, :half], key_proj, gain_columns], axis=1),
        jnp.concatenate([query_proj[:, half:], value_proj, gain_columns], axis=1),
    )
    out_ordered = ordered(attn_out).astype(BF16)
    out_halves = out_ordered[:, : width // 2], out_ordered[:, width // 2 :]
    qkv_width = half + head_size
    ff_unit = first_down.shape[0]
    lru_unit = mixer_out.shape[0]

    block_width = rate_gate.shape[1]
    tap_count = conv_taps.shape[1]
    spare = block_width - tap_count - 1
    second_chip = chip_rows(*split_columns((second_gate, second_up), ff_unit, reps))
    qkv_halves, second_chip = lax.optimization_barrier((qkv_halves, second_chip))
    second_in_w = gather_plain(second_chip, True)
    qkv_own, attn_own, first_in_w, first_down_w, lru_in_w, small_w, mix_w, second_down_w = gather_all(
        (
            chip_rows(by_core(*qkv_halves), by_core(*qkv_halves[::-1])),
            chip_rows(by_core(*out_halves), by_core(*out_halves[::-1])),
            chip_rows(*split_columns((first_gate, first_up), ff_unit, reps)),
            ordered(first_down).astype(BF16),
            chip_rows(*split_columns((branch_proj, gated_proj), lru_unit)),
            jnp.concatenate(
                [
                    rate_gate,
                    input_gate,
                    conv_taps,
                    decay_rate[:, None],
                    jnp.zeros((lru_unit, spare), BF16),
                ],
                axis=1,
            ),
            ordered(mixer_out).astype(BF16),
            ordered(second_down).astype(BF16),
        ),
        (True, True, True, True, True, False, False, True),
        (1024, 768, 1536, 1536, 1024, 384, 1536, 1536),
    )
    gains = qkv_own[:, qkv_width:].astype(F32)
    gain_attn, gain_first, gain_mix, gain_second = (gains[:, i] for i in range(4))
    qkv_sib = swap_cores(qkv_own)
    attn_sib = swap_cores(attn_own)

    inputs = ordered(tokens_in.reshape(row_count, width))
    attn_normed = rms_norm(inputs, gain_attn).astype(BF16)
    qkv_mine = matmul(attn_normed, qkv_own).astype(BF16)
    qkv_other = matmul(attn_normed, qkv_sib).astype(BF16)
    qkv_first, qkv_second = by_core(qkv_mine, qkv_other), by_core(qkv_other, qkv_mine)
    query_rows = jnp.concatenate([qkv_first[:, :half], qkv_second[:, :half]], axis=1)
    kv_rows = jnp.concatenate(
        [qkv_first[:, half:qkv_width], qkv_second[:, half:qkv_width]], axis=1
    )
    blocks_behind = -(-WINDOW // row_count)
    behind = blocks_behind * row_count
    kv_win = jnp.concatenate(
        [shift_rep(kv_rows, by) for by in range(blocks_behind, 0, -1) if by < reps]
        + [kv_rows],
        axis=0,
    )
    behind = kv_win.shape[0] - row_count
    (attended,) = attention_call(
        attention_kernel,
        start_row,
        [query_rows],
        kv_win,
        [jax.ShapeDtypeStruct((row_count, width), BF16)],
    )
    attended_low = ordered(attended).astype(BF16)
    out_mine = matmul(attended_low, attn_own)
    out_other = matmul(attended_low, attn_sib)
    resid_one = inputs + jnp.concatenate(
        [by_core(out_mine, out_other), by_core(out_other, out_mine)], axis=1
    )

    middle, first_kept = mlp_forward(resid_one, gain_first, first_in_w, first_down_w)

    conv_w = small_w[:, 2 * block_width : 2 * block_width + tap_count].astype(F32).T
    decay_w = small_w[:, 2 * block_width + tap_count].astype(F32)[None]
    rate_w = small_w[:, :block_width]
    input_w = small_w[:, block_width : 2 * block_width]
    mix_normed = with_sibling(rms_norm(middle, gain_mix).astype(BF16))
    lru_width = lru_in_w.shape[1] // 2
    branch_gated = matmul(mix_normed, lru_in_w).reshape(2, row_count, 2 * lru_width)
    tail_rows = shift_rep(branch_gated[:, row_count - 8 :, :lru_width], 1)
    lru_inputs = [
        (branch_gated, "first"),
        (tail_rows, "edge"),
        (rate_w, "weight"),
        (input_w, "weight"),
        (conv_w, "taps"),
        (decay_w, "row"),
    ]
    wide = (jax.ShapeDtypeStruct((2, row_count, lru_width), F32), "first")
    wide_low = (jax.ShapeDtypeStruct((2, row_count, lru_width), BF16), "first")
    edge = (jax.ShapeDtypeStruct((2, 8, lru_width), F32), "edge")
    scans = [pltpu.VMEM((row_count, 256), F32)] * 2
    lru_coef, cum_coef, local_state, cum_last, state_last = lru_call(
        functools.partial(lru_forward_kernel, block_width),
        lru_inputs,
        [wide, wide, wide, edge, edge],
        row_count,
        scans,
    )
    start_state = carried_in(cum_last[:, 7], state_last[:, 7], False)
    start_edge = jnp.broadcast_to(start_state[:, None], edge[0].shape)
    gated_act = gelu_tanh(branch_gated[:, :, lru_width:])
    mix_low = ((local_state + cum_coef * start_state[:, None]) * gated_act).astype(BF16)
    mix_low = mix_low.reshape(2 * row_count, lru_width)
    resid_two = middle + sum_parts(matmul(mix_low, mix_w))

    final_rows, second_kept = mlp_forward(
        resid_two, gain_second, second_in_w, second_down_w
    )
    out_tokens = unordered(final_rows.astype(BF16)).astype(BF16).reshape(1, row_count, width)
    back_final = ordered(cotangent.reshape(row_count, width)) * valid_mask
    back_two, second_grads = mlp_backward(
        resid_two,
        gain_second,
        second_in_w,
        second_down_w,
        second_kept,
        back_final,
    )

    down_part = lax.psum_scatter(
        matmul_left(*second_grads[3]).astype(BF16), "rep", scatter_dimension=0, tiled=True
    )
    in_part = lax.psum_scatter(
        matmul_left(
            second_grads[1][0],
            jnp.concatenate([second_grads[1][1], second_grads[2][1]], axis=1),
        ).astype(BF16),
        "rep",
        scatter_dimension=0,
        tiled=True,
    )

    mix_back_low = with_sibling(back_two.astype(BF16))
    back_mixed = matmul_right(mix_back_low, mix_w).astype(BF16).reshape(wide[0].shape)
    later_prod, local_adjoint, gated_back_low, out_first = lru_call(
        lru_adjoint_kernel,
        [
            (branch_gated, "second"),
            (lru_coef, "first"),
            (cum_coef, "first"),
            (local_state, "first"),
            (start_edge, "edge"),
            (back_mixed, "first"),
        ],
        [wide, wide, wide_low, edge],
        row_count,
        scans,
    )
    gated_back_low = gated_back_low.reshape(2 * row_count, lru_width)
    carry_in = carried_in(cum_last[:, 7], out_first[:, 0], True)
    carry_edge = jnp.broadcast_to(carry_in[:, None], edge[0].shape)
    branch_back, first_rows, last_rows, grad_rate, grad_input, grad_taps, grad_decay = lru_call(
        functools.partial(lru_backward_kernel, block_width),
        lru_inputs
        + [
            (cum_coef, "first"),
            (local_state, "first"),
            (start_edge, "edge"),
            (later_prod, "first"),
            (local_adjoint, "first"),
            (carry_edge, "edge"),
        ],
        [
            wide_low,
            edge,
            edge,
            (jax.ShapeDtypeStruct((lru_width, block_width), F32), "weight"),
            (jax.ShapeDtypeStruct((lru_width, block_width), F32), "weight"),
            (jax.ShapeDtypeStruct((tap_count, lru_width), F32), "taps"),
            (jax.ShapeDtypeStruct((1, lru_width), F32), "row"),
        ],
        row_count,
    )
    spill = jnp.concatenate([jnp.zeros_like(first_rows), shift_rep(first_rows, -1)], axis=1)
    for j in range(1, tap_count):
        last_rows = last_rows + conv_w[j] * spill[:, j : j + 8]
    branch_back_low = lax.dynamic_update_slice_in_dim(
        branch_back, last_rows.astype(BF16), row_count - 8, 1
    ).reshape(2 * row_count, lru_width)
    back_mix_normed = sum_parts(
        matmul_right(jnp.concatenate([branch_back_low, gated_back_low], axis=1), lru_in_w)
    )
    back_middle_norm, grad_mix_gain = jax.vjp(rms_norm, middle, gain_mix)[1](back_mix_normed)
    back_middle, down_part = lax.optimization_barrier((back_two + back_middle_norm, down_part))
    down_part = lax.psum_scatter(
        down_part, "shard", scatter_dimension=0, tiled=True, axis_index_groups=chip_groups()
    )
    grad_small = jnp.concatenate(
        [
            grad_rate.astype(BF16),
            grad_input.astype(BF16),
            grad_taps.T.astype(BF16),
            grad_decay.T.astype(BF16),
            jnp.zeros((lru_width, spare), BF16),
        ],
        axis=1,
    )

    back_one, first_grads = mlp_backward(
        resid_one, gain_first, first_in_w, first_down_w, first_kept, back_middle
    )

    attn_back_low, in_part = lax.optimization_barrier((back_one.astype(BF16), in_part))
    in_part = lax.psum_scatter(
        in_part, "shard", scatter_dimension=0, tiled=True, axis_index_groups=chip_groups()
    )
    back_halves = attn_back_low[:, : width // 2], attn_back_low[:, width // 2 :]
    back_mine, back_other = by_core(*back_halves), by_core(back_halves[1], back_halves[0])
    attended_both = with_sibling(attended_low)
    out_right = jnp.concatenate([back_mine, swap_cores(back_other)], axis=0)
    back_attended = matmul_right(back_mine, attn_own) + matmul_right(back_other, attn_sib)
    back_attended = unordered(back_attended.astype(BF16)).astype(BF16)
    back_query, back_kv_win = attention_call(
        attention_back_kernel,
        start_row,
        [query_rows, back_attended],
        kv_win,
        [
            jax.ShapeDtypeStruct((row_count, width), BF16),
            jax.ShapeDtypeStruct(kv_win.shape, F32),
        ],
    )
    back_kv = back_kv_win[behind:]
    for by in range(1, behind // row_count + 1):
        begin = behind - by * row_count
        back_kv = back_kv + shift_rep(back_kv_win[begin : begin + row_count], -by)
    back_kv = back_kv.astype(BF16)
    back_first = jnp.concatenate([back_query[:, :half], back_kv[:, :head_size]], axis=1)
    back_second = jnp.concatenate([back_query[:, half:], back_kv[:, head_size:]], axis=1)
    qkv_back_mine = by_core(back_first, back_second)
    qkv_back_other = by_core(back_second, back_first)
    gain_pad = ((0, 0), (0, 128))
    back_attn_normed = matmul_right(jnp.pad(qkv_back_mine, gain_pad), qkv_own) + matmul_right(
        jnp.pad(qkv_back_other, gain_pad), qkv_sib
    )
    back_inputs_norm, grad_attn_gain = jax.vjp(rms_norm, inputs, gain_attn)[1](back_attn_normed)
    input_grad = (
        unordered((back_one + back_inputs_norm).astype(BF16))
        .astype(BF16)
        .reshape(1, row_count, width)
    )

    gain_given = jnp.stack([grad_attn_gain, first_grads[0], grad_mix_gain, second_grads[0]])
    gain_given = jnp.pad(gain_given, ((0, 124), (0, 0))).astype(BF16).T.reshape(reps, -1, 128)
    qkv_right = jnp.concatenate([qkv_back_mine, swap_cores(qkv_back_other)], axis=0)
    def by_reps(x):
        parts = x.reshape(chips, reps, -1, x.shape[1]).transpose(1, 0, 2, 3)
        return parts.reshape(reps, -1, x.shape[1])

    sub = lru_unit // reps
    spot = lax.broadcasted_iota(jnp.int32, (lru_width, lru_width), 1)
    source = (
        lax.rem(spot // sub, chips) * lru_unit + (spot // (sub * chips)) * sub + lax.rem(spot, sub)
    )
    to_reps = lax.broadcasted_iota(jnp.int32, (lru_width, lru_width), 0) == source
    mix_by_reps = matmul(mix_low, to_reps.astype(BF16)).astype(BF16)
    lru_in, first_in, first_down_rows, qkv_rows, out_rows, gain_rows, mix_rows, small_rows = (
        reduce_all(
            [
                (mix_normed, [branch_back_low, gated_back_low], 512),
                (first_grads[1][0], [first_grads[1][1], first_grads[2][1]], 768),
                (first_grads[3][0], [first_grads[3][1]], 512),
                (with_sibling(attn_normed), [qkv_right], 512),
                (with_sibling(attended_low), [out_right], 768),
                (None, [gain_given], 128),
                (mix_by_reps, [mix_back_low], 768),
                (None, [by_reps(grad_small)], 384),
            ]
        )
    )

    lru_in, in_part, down_part = lax.optimization_barrier((lru_in, in_part, down_part))
    second_in = lax.all_gather(in_part, "rep", axis=0, tiled=True)
    second_down_rows = lax.all_gather(down_part, "rep", axis=0, tiled=True)
    grad_mixer_out = unordered(mix_rows)
    small = small_rows.astype(F32)

    def in_reduced(reduced, unit, parts=1):
        return join_columns(*own_rows(reduced), 2, unit, parts)

    grad_second_gate, grad_second_up = in_reduced(second_in, ff_unit, reps)
    grad_second_down = unordered(second_down_rows)
    grad_branch_proj, grad_gated_proj = in_reduced(lru_in, lru_unit)
    grad_first_gate, grad_first_up = in_reduced(first_in, ff_unit, reps)
    grad_first_down = unordered(first_down_rows)
    qkv_mine, qkv_other = own_rows(qkv_rows)
    grad_query = jnp.concatenate(
        [by_core(qkv_mine, qkv_other)[:, :half], by_core(qkv_other, qkv_mine)[:, :half]], axis=1
    ).astype(F32)
    grad_key = by_core(qkv_mine, qkv_other)[:, half:].astype(F32)
    grad_value = by_core(qkv_other, qkv_mine)[:, half:].astype(F32)
    out_mine, out_other = own_rows(out_rows)
    grad_out_proj = unordered(
        jnp.concatenate([by_core(out_mine, out_other), by_core(out_other, out_mine)], axis=1)
    )
    gain_mine, gain_other = own_rows(gain_rows)
    gain_grads = (gain_mine.astype(F32) + gain_other.astype(F32)).T
    return (
        out_tokens,
        input_grad,
        gain_grads[0],
        grad_query,
        grad_key,
        grad_value,
        grad_out_proj,
        gain_grads[1],
        grad_first_gate,
        grad_first_up,
        grad_first_down,
        gain_grads[2],
        grad_branch_proj,
        grad_gated_proj,
        small[:, 2 * block_width : 2 * block_width + tap_count],
        small[:, :block_width],
        small[:, block_width : 2 * block_width],
        small[:, 2 * block_width + tap_count],
        grad_mixer_out,
        gain_grads[3],
        grad_second_gate,
        grad_second_up,
        grad_second_down,
    )


def solution(mesh):
    rows = P("shard", None)
    vector = P("shard")
    tokens = P("shard", "rep", None)
    weights = (
        vector,
        rows,
        rows,
        rows,
        rows,
        vector,
        rows,
        rows,
        rows,
        vector,
        rows,
        rows,
        rows,
        rows,
        rows,
        vector,
        rows,
        vector,
        rows,
        rows,
        rows,
    )
    return jax.shard_map(
        on_device,
        mesh=mesh,
        in_specs=(tokens, vector, tokens) + weights,
        out_specs=(tokens, tokens) + weights,
        check_vma=False,
    )
```
